128 devices in a mesh: dp: 4 (over x), ctx: 32 (over z, y, core).
Axes of the slice: x: 4, y: 4, z: 4, core: 2. Of those that a mesh axis runs over, the one named last changes fastest.
Arguments:
- segment_ids: int32 [32768], P(('dp', 'ctx')), parts along dimension 0, may hold values from 0 to 7, never falling along the last dimension, each value on 1 to 4096 neighbouring positions
- attn_query: bfloat16 [32768, 2048], P(('dp', 'ctx')), parts along dimension 0, may hold values from -96 to 96
- attention_keys: bfloat16 [32768, 256], P(('dp', 'ctx')), parts along dimension 0, may hold values from -8 to 8
- attention_values: bfloat16 [32768, 256], P(('dp', 'ctx')), parts along dimension 0, may hold values from -6 to 6
- attn_gate: bfloat16 [32768, 2048], P(('dp', 'ctx')), parts along dimension 0, may hold values from -8 to 8
- delta_query: bfloat16 [32768, 1024], P(('dp', 'ctx')), parts along dimension 0, may hold values from -400 to 400
- delta_key: bfloat16 [32768, 1024], P(('dp', 'ctx')), parts along dimension 0, may hold values from -400 to 400
- update_rule_payload: bfloat16 [32768, 2048], P(('dp', 'ctx')), parts along dimension 0, may hold values from -400 to 400
- delta_beta: float32 [32768, 16], P(('dp', 'ctx')), parts along dimension 0, may hold values from 0.1 to 0.9
- delta_decay: float32 [32768, 16], P(('dp', 'ctx')), parts along dimension 0, may hold values from -1 to 0
- delta_gate: bfloat16 [32768, 2048], P(('dp', 'ctx')), parts along dimension 0, may hold values from -8 to 8
- norm_gain: float32 [128], replicated, may hold values from 0.5 to 1.5
Outputs:
- attn_mixed: bfloat16 [32768, 2048], P(('dp', 'ctx')), parts along dimension 0
- delta_mixed: bfloat16 [32768, 2048], P(('dp', 'ctx')), parts along dimension 0
The draws below stay inside these ranges and needn't reach their ends.
There are 4 independent parts, one for each index of `dp`. The reference program is written for one: setup_inputs(seed, part) draws one part's arguments, and reference() takes and returns one part's arrays. A program takes and returns all parts, laid end to end along the dimension named above; an argument that names none is the same for every part. Nothing has to cross between parts.
Inputs may be any that keep to these rules, and one draw needn't show every extreme that they name: `segment_ids`: segment ids never fall along the sequence; each of the 8 documents holds 1 to 4096 positions, and one holds exactly 4096.
All inputs are finite; a program needn't handle non-finite values.
Results may differ from the reference program's by a relative error of at most 0.0085.
Values may be sent and summed in bfloat16 or wider, within the bound.
A program may use at most 256 MiB of HBM per device.

```python
import math
import jax
import jax.numpy as jnp
import numpy as np
from jax import lax

QUERY_HEADS = 8
KEY_VALUE_HEADS = 1
HEAD_WIDTH = 256
ROTARY_ENTRIES = 64
HK = 8
HV = 16
DK = 128
DV = 128
GROUP = 2
DOCS = 8
TOK_DEV = 256
TOKEN_SPAN_TOTAL = 8192


def attention_pair(key):
    query_vector = jax.random.normal(jax.random.fold_in(key, 101), (TOKEN_SPAN_TOTAL, QUERY_HEADS, HEAD_WIDTH), jnp.float32)
    key_rows = jax.random.normal(jax.random.fold_in(key, 102), (TOKEN_SPAN_TOTAL, KEY_VALUE_HEADS, HEAD_WIDTH), jnp.float32)
    return (jnp.clip(query_vector, -96.0, 96.0).reshape(TOKEN_SPAN_TOTAL, QUERY_HEADS * HEAD_WIDTH), jnp.clip(key_rows, -8.0, 8.0).reshape(TOKEN_SPAN_TOTAL, KEY_VALUE_HEADS * HEAD_WIDTH))


def draw_attn_query(key, part):
    return attention_pair(key)[0].astype(jnp.bfloat16)


def draw_attention_keys(key, part):
    return attention_pair(key)[1].astype(jnp.bfloat16)


def scaled_rows(key, width):
    reach = jnp.log(10.0)
    base = jnp.clip(jax.random.normal(jax.random.fold_in(key, 1), (TOKEN_SPAN_TOTAL, width), jnp.float32), -4.5, 4.5)
    row_scale = jnp.exp(jax.random.uniform(jax.random.fold_in(key, 3), (TOKEN_SPAN_TOTAL, 1), jnp.float32, 0.0, reach))
    column_scale = jnp.exp(jax.random.uniform(jax.random.fold_in(key, 4), (1, width), jnp.float32, 0.0, reach))
    return jnp.clip(0.25 * base * row_scale * column_scale, -400.0, 400.0)


def draw_delta_query(key, part):
    return scaled_rows(jax.random.fold_in(key, 201), HK * DK).astype(jnp.bfloat16)


def draw_delta_key(key, part):
    return scaled_rows(jax.random.fold_in(key, 202), HK * DK).astype(jnp.bfloat16)


def draw_update_rule_payload(key, part):
    return scaled_rows(jax.random.fold_in(key, 203), HV * DV).astype(jnp.bfloat16)


def draw_delta_decay(key, part):
    order = jax.random.permutation(jax.random.fold_in(key, 301), HV)
    slow_count = HV // 2
    slow_rate = -0.5 / TOKEN_SPAN_TOTAL
    slow = (order < slow_count)[None, :]
    fast_rate = -1.0 / jax.random.uniform(jax.random.fold_in(key, 302), (1, HV), jnp.float32, 30.0, 50.0)
    rate = jnp.where(slow, slow_rate, fast_rate)
    blocks = TOKEN_SPAN_TOTAL // TOK_DEV
    factor = jnp.exp(jax.random.uniform(jax.random.fold_in(key, 303), (blocks, HV), jnp.float32, jnp.log(0.6), jnp.log(1.3)))
    factor_rows = jnp.repeat(factor, TOK_DEV, axis=0)
    jitter = jax.random.uniform(jax.random.fold_in(key, 304), (TOKEN_SPAN_TOTAL, HV), jnp.float32, 0.5, 1.5)
    episode_offset = jax.random.randint(jax.random.fold_in(key, 305), (2,), 0, TOKEN_SPAN_TOTAL)
    slot_number = jnp.arange(TOKEN_SPAN_TOTAL)
    blocked_pattern = jnp.any(slot_number[:, None] == episode_offset[None, :], axis=1)
    loss = jnp.log(jax.random.uniform(jax.random.fold_in(key, 306), (TOKEN_SPAN_TOTAL, HV), jnp.float32, 0.5, 0.8))
    decay = rate * factor_rows * jitter + jnp.where(blocked_pattern[:, None], loss, 0.0)
    return jnp.clip(decay, -1.0, 0.0)


def level_of(key, dims, split, smallest, high):
    loudness = 1.0
    for position, shards_of in split:
        steps = jax.random.uniform(jax.random.fold_in(jax.random.fold_in(key, 6), position), (shards_of,), jnp.float32, smallest / len(split), high / len(split))
        loudness = loudness * jnp.repeat(jnp.exp(steps), dims[position] // shards_of).reshape((-1,) + (1,) * (len(dims) - 1 - position))
    return loudness


def split_up(amount, total, limit, skew):
    weights = [(1 << 20) // math.isqrt(standing ** skew) + 1 for standing in range(2, amount + 1)]
    surplus, holding = total - limit - (amount - 1), [1] * (amount - 1)
    while surplus > 0:
        movable = [i for i in range(amount - 1) if holding[i] < limit]
        mass, left = sum([weights[i] for i in movable]), surplus
        for i in movable:
            more = min(limit - holding[i], max(1, left * weights[i] // mass), surplus)
            holding[i] = holding[i] + more
            surplus = surplus - more
    return np.array([limit] + holding)


def ragged(rng, number_of, total, bound, skew):
    if number_of == 2:
        one = jax.random.randint(rng, (), max(1, total - bound), min(bound, total - 1) + 1)
        return jnp.stack([one, total - one])
    sizes = jnp.asarray(split_up(number_of, total, bound, skew), jnp.int32)
    pairs = (number_of - 1) // 2
    source_of, receiver = sizes[1:1 + 2 * pairs:2], sizes[2:2 + 2 * pairs:2]
    margin = jnp.minimum(source_of - 1, bound - receiver)
    moved = jax.random.randint(jax.random.fold_in(rng, 1), (pairs,), 0, 1 << 20) % (margin + 1)
    sizes = sizes.at[1:1 + 2 * pairs:2].set(source_of - moved).at[2:2 + 2 * pairs:2].set(receiver + moved)
    return sizes[jax.random.permutation(jax.random.fold_in(rng, 2), number_of)]


def gaussian(own_key, shape, scale, bound, pieces=(), kind=jnp.bfloat16):
    gain = level_of(own_key, shape, pieces, -0.22, 0.18) if pieces else 1.0
    array = jax.random.normal(own_key, shape, jnp.float32) * scale * gain
    return jnp.minimum(jnp.maximum(array, -bound), bound).astype(kind)


def setup_inputs(seed: int = 0, part: int = 0) -> dict:
    streams_of = jax.random.split(jax.random.key(seed), 13)
    own_keys = jax.random.split(jax.random.fold_in(streams_of[12], part), 13)
    segment_ids = jnp.searchsorted(jnp.cumsum(ragged(own_keys[0], DOCS, TOKEN_SPAN_TOTAL, TOKEN_SPAN_TOTAL // 2, 0)), jnp.arange(TOKEN_SPAN_TOTAL), side="right").astype(jnp.int32)
    attn_query = draw_attn_query(jax.random.fold_in(jax.random.fold_in(streams_of[12], part), 71), part)
    attention_keys = draw_attention_keys(jax.random.fold_in(jax.random.fold_in(streams_of[12], part), 71), part)
    attention_values = gaussian(own_keys[3], (TOKEN_SPAN_TOTAL, KEY_VALUE_HEADS * HEAD_WIDTH), 1.0, 6.0, ((0, 32),))
    attn_gate = gaussian(own_keys[4], (TOKEN_SPAN_TOTAL, QUERY_HEADS * HEAD_WIDTH), 1.5, 8.0, ((0, 32),))
    delta_query = draw_delta_query(jax.random.fold_in(jax.random.fold_in(streams_of[12], part), 71), part)
    delta_key = draw_delta_key(jax.random.fold_in(jax.random.fold_in(streams_of[12], part), 71), part)
    update_rule_payload = draw_update_rule_payload(jax.random.fold_in(jax.random.fold_in(streams_of[12], part), 71), part)
    delta_beta = jnp.clip(0.1 + 0.79999997 * jax.random.uniform(own_keys[8], (TOKEN_SPAN_TOTAL, HV), jnp.float32) ** level_of(own_keys[8], (TOKEN_SPAN_TOTAL, HV), ((0, 32),), -0.2, 0.2), 0.1, 0.9)
    delta_decay = draw_delta_decay(jax.random.fold_in(jax.random.fold_in(streams_of[12], part), 71), part)
    delta_gate = gaussian(own_keys[10], (TOKEN_SPAN_TOTAL, HV * DV), 1.5, 8.0, ((0, 32),))
    norm_gain = jnp.clip(1.0 + 0.1 * jax.random.normal(streams_of[11], (DV,), jnp.float32), 0.5, 1.5)
    return dict(segment_ids=segment_ids, attn_query=attn_query, attention_keys=attention_keys, attention_values=attention_values, attn_gate=attn_gate, delta_query=delta_query, delta_key=delta_key, update_rule_payload=update_rule_payload, delta_beta=delta_beta, delta_decay=delta_decay, delta_gate=delta_gate, norm_gain=norm_gain)


rope_theta = 10000000.0

def apply_rotary(field, shift_amount):
    half = ROTARY_ENTRIES // 2
    index = jnp.arange(half).astype(jnp.float32)
    freq = rope_theta ** (-2.0 * index / ROTARY_ENTRIES)
    angle = shift_amount.astype(jnp.float32)[:, None, None] * freq[None, None, :]
    angular_cos_table = jnp.cos(angle)
    sine = jnp.sin(angle)
    first = field[..., :half]
    second = field[..., half:ROTARY_ENTRIES]
    return jnp.concatenate([first * angular_cos_table - second * sine, second * angular_cos_table + first * sine, field[..., ROTARY_ENTRIES:]], axis=-1)

def normalize(field):
    return field * lax.rsqrt(lax.optimization_barrier(jnp.sum(field * field, axis=-1, keepdims=True)) + 1e-06)

def reference(segment_ids, attn_query, attention_keys, attention_values, attn_gate, delta_query, delta_key, update_rule_payload, delta_beta, delta_decay, delta_gate, norm_gain):
    slot_number = jnp.arange(TOKEN_SPAN_TOTAL, dtype=jnp.int32)
    boundary = jnp.concatenate([jnp.ones((1,), dtype=bool), segment_ids[1:] != segment_ids[:-1]])
    starts = lax.cummax(jnp.where(boundary, slot_number, 0), axis=0)
    shift_amount = slot_number - starts
    query_vector = apply_rotary(attn_query.astype(jnp.float32).reshape(TOKEN_SPAN_TOTAL, QUERY_HEADS, HEAD_WIDTH), shift_amount).astype(jnp.bfloat16)
    key_rows = apply_rotary(attention_keys.astype(jnp.float32).reshape(TOKEN_SPAN_TOTAL, KEY_VALUE_HEADS, HEAD_WIDTH), shift_amount).astype(jnp.bfloat16)
    value_matrix = attention_values.reshape(TOKEN_SPAN_TOTAL, KEY_VALUE_HEADS, HEAD_WIDTH)
    gates = jax.nn.sigmoid(attn_gate.astype(jnp.float32)).reshape(TOKEN_SPAN_TOTAL, QUERY_HEADS, HEAD_WIDTH)
    allowed = (slot_number[None, :] <= slot_number[:, None]) & (slot_number[None, :] >= starts[:, None])
    shared_portion = QUERY_HEADS // KEY_VALUE_HEADS
    heads = []
    for head in range(QUERY_HEADS):
        scores = jnp.dot(query_vector[:, head], key_rows[:, head // shared_portion].T, preferred_element_type=jnp.float32) * HEAD_WIDTH ** (-0.5)
        scores = jnp.where(allowed, scores, -jnp.inf)
        highest_score = lax.optimization_barrier(jnp.max(scores, axis=1, keepdims=True))
        weights = jnp.where(allowed, jnp.exp(scores - highest_score), 0.0)
        total = lax.optimization_barrier(jnp.sum(weights, axis=1, keepdims=True))
        mixed = jnp.dot(weights.astype(jnp.bfloat16), value_matrix[:, head // shared_portion], preferred_element_type=jnp.float32)
        heads.append(mixed / total * gates[:, head])
    attn_mixed = jnp.stack(heads, axis=1).reshape(TOKEN_SPAN_TOTAL, QUERY_HEADS * HEAD_WIDTH).astype(jnp.bfloat16)
    unit_query = normalize(delta_query.astype(jnp.float32).reshape(TOKEN_SPAN_TOTAL, HK, DK)) * DK ** (-0.5)
    unit_key = normalize(delta_key.astype(jnp.float32).reshape(TOKEN_SPAN_TOTAL, HK, DK))
    unit_query = jnp.repeat(unit_query, GROUP, axis=1)
    unit_key = jnp.repeat(unit_key, GROUP, axis=1)
    value_rows = update_rule_payload.astype(jnp.float32).reshape(TOKEN_SPAN_TOTAL, HV, DV)
    retain = jnp.exp(delta_decay) * (shift_amount != 0).astype(jnp.float32)[:, None]

    def advance(recurrent_state, inputs):
        query_entry, key_vector, value_row, beta_row, retain_row = inputs
        recurrent_state = retain_row[:, None, None] * recurrent_state
        estimate = jnp.einsum('cmp,cm->cp', recurrent_state, key_vector, precision=lax.Precision.HIGHEST)
        recurrent_state = recurrent_state + key_vector[:, :, None] * (beta_row[:, None] * (value_row - estimate))[:, None, :]
        return (recurrent_state, jnp.einsum('cmp,cm->cp', recurrent_state, query_entry, precision=lax.Precision.HIGHEST))
    final_state, outputs = lax.scan(advance, jnp.zeros((HV, DK, DV), jnp.float32), (unit_query, unit_key, value_rows, delta_beta, retain))
    spread = lax.rsqrt(lax.optimization_barrier(jnp.mean(outputs * outputs, axis=-1, keepdims=True)) + 1e-06)
    gate_rows = jax.nn.silu(delta_gate.astype(jnp.float32).reshape(TOKEN_SPAN_TOTAL, HV, DV))
    delta_mixed = (outputs * spread * norm_gain * gate_rows).reshape(TOKEN_SPAN_TOTAL, HV * DV).astype(jnp.bfloat16)
    return (attn_mixed, delta_mixed)
```

```python
import functools

import jax
import jax.numpy as jnp
from jax import lax
from jax.experimental import pallas as pl
from jax.experimental.pallas import tpu as pltpu
from jax.sharding import PartitionSpec as P

HEAD_WIDTH = 256
ROTARY_ENTRIES = 64
ROPE_THETA = 10000000.0
DK = 128
DOCS = 8
ROWS = 256
RANKS = 32
SLOTS = 17
HEADS_Q = 8
HEADS_K = 8
HEADS_V = 16
GROUPS = 4
PER = HEADS_K // GROUPS
MESH = pl.DeviceIdType.MESH
F32 = jnp.float32
BF16 = jnp.bfloat16
NEG = -1e30


def nn(a, b):
    return lax.dot_general(a, b, (((1,), (0,)), ((), ())), preferred_element_type=F32)


def nt(a, b):
    return lax.dot_general(a, b, (((1,), (1,)), ((), ())), preferred_element_type=F32)


def tn(a, b):
    return lax.dot_general(a, b, (((0,), (0,)), ((), ())), preferred_element_type=F32)


def iota(shape, dim):
    return lax.broadcasted_iota(jnp.int32, shape, dim)


def lanes(index, width):
    return pl.ds(pl.multiple_of(index * width, width), width)


def rotate(x, cos, sin):
    lane = iota(x.shape, 1)
    swapped = jnp.where(lane < 32, pltpu.roll(x, 96, 1), pltpu.roll(x, 32, 1))
    return x * cos + swapped * sin


def pair_diag(packed):
    zero = jnp.zeros((128, 128), packed.dtype)
    return jnp.concatenate(
        [
            jnp.concatenate([packed[:, :128], zero], axis=1),
            jnp.concatenate([zero, packed[:, 128:]], axis=1),
        ],
        axis=0,
    )


def inverse(lower):
    row = iota((128, 256), 0)
    col = iota((128, 256), 1) % 128
    apart = row ^ col
    packed = jnp.concatenate([lower[:128, :128], lower[128:, 128:]], axis=1)
    inv = jnp.where(apart == 0, 1.0, 0.0) - jnp.where(apart == 1, packed, 0.0)
    block = 2
    while block < 128:
        here = (apart >= block) & (apart < 2 * block)
        off = jnp.where(here, packed, 0.0).astype(BF16)
        inv_b = inv.astype(BF16)
        left = nn(inv_b, pair_diag(off)).astype(BF16)
        inv = inv - nn(left, pair_diag(inv_b))
        block *= 2
    inv_b = inv.astype(BF16)
    first, second = inv_b[:, :128], inv_b[:, 128:]
    corner = nn(second, nn(lower[128:, :128].astype(BF16), first).astype(BF16))
    return jnp.concatenate(
        [
            jnp.concatenate([first, jnp.zeros((128, 128), BF16)], axis=1),
            jnp.concatenate([(-corner).astype(BF16), second], axis=1),
        ],
        axis=0,
    )


def kernel(
    seg_col, seg_row, freq, q, k, v, gate, dq, dk, pv, beta, decay, dgate, gain,
    attn_out, delta_out,
    cnt, counts, kv, colg, colb, row_pack, mta, reach, intra, inbox, stage, state_in,
    qr, s_buf, tables, state,
    cnt_send, cnt_recv, kv_send, kv_recv, mta_send, mta_recv, st_send, st_recv,
):
    me = lax.axis_index("ctx")
    core = lax.rem(me, 2)
    chip = me // 2
    y = lax.rem(chip, 4)
    z = chip // 4

    def at(zz, yy, cc):
        return {"ctx": (lax.rem(zz, 4) * 4 + lax.rem(yy, 4)) * 2 + cc}

    barrier = pltpu.get_barrier_semaphore()

    @pl.loop(1, RANKS)
    def _(j):
        pl.semaphore_signal(
            barrier, inc=1, device_id={"ctx": lax.rem(me + j, RANKS)}, device_id_type=MESH
        )

    pl.semaphore_wait(barrier, RANKS - 1)

    lane1 = iota((ROWS, 128), 1)
    seg = seg_col[...]
    mine = jnp.sum(jnp.where(seg == lane1, 1.0, 0.0), axis=0, keepdims=True)
    cnt[...] = jnp.broadcast_to(mine, (8, 128))
    counts[0] = jnp.broadcast_to(mine, (8, 128))

    @pl.loop(1, RANKS)
    def _(j):
        pltpu.make_async_remote_copy(
            cnt, counts.at[j], cnt_send, cnt_recv,
            device_id={"ctx": lax.rem(me + j, RANKS)}, device_id_type=MESH,
        ).start()

    pack = jnp.zeros((ROWS, 128), F32)
    triangle = jnp.where(iota((ROWS, ROWS), 0) >= iota((ROWS, ROWS), 1), 1.0, 0.0).astype(BF16)
    dec = decay[...]
    hi = dec.astype(BF16)
    mid = (dec - hi.astype(F32)).astype(BF16)
    low = (dec - hi.astype(F32) - mid.astype(F32)).astype(BF16)
    sums = nn(triangle, hi) + nn(triangle, mid) + nn(triangle, low)
    bet = beta[...]
    for g in range(GROUPS):
        w = 2 * PER
        colg[g, :, :w] = sums[:, g * w : (g + 1) * w]
        colb[g, :, :w] = bet[:, g * w : (g + 1) * w]
    pack = jnp.concatenate([sums, jnp.zeros((ROWS, 112), F32)], axis=1)
    for h in range(HEADS_K):
        kf = dk[:, h * DK : (h + 1) * DK].astype(F32)
        rk = lax.rsqrt(jnp.sum(kf * kf, axis=1, keepdims=True) + 1e-06)
        pack = jnp.where(lane1 == 16 + h, rk, pack)
    row_pack[...] = pack.T

    pltpu.make_async_copy(counts.at[pl.ds(1, RANKS - 1)], counts.at[pl.ds(1, RANKS - 1)], cnt_recv).wait()
    totals = jnp.sum(counts[...], axis=0)[0:1]
    starts = jnp.sum(jnp.where(lane1 < seg, totals, 0.0), axis=1, keepdims=True)
    slot = (me * ROWS).astype(F32) + iota((ROWS, 1), 0).astype(F32)
    angle = (slot - starts) * freq[...]
    sign = jnp.where(lane1 < 32, -1.0, 1.0)
    cos = jnp.cos(angle)
    sin = jnp.sin(angle) * sign
    tables[0] = cos
    tables[1] = sin
    kv[0, 0, :, :128] = rotate(k[:, :128].astype(F32), cos, sin).astype(BF16)
    kv[0, 0, :, 128:] = k[:, 128:]
    kv[0, 1] = v[...]

    def send_kv(src, dst, target):
        pltpu.make_async_remote_copy(
            kv.at[src], kv.at[dst], kv_send, kv_recv.at[dst], device_id=target, device_id_type=MESH
        ).start()

    def got_kv(j):
        pltpu.make_async_copy(kv.at[j], kv.at[j], kv_recv.at[j]).wait()

    def to_twin(d):
        send_kv(2 * d, 2 * d + 1 - 2 * core, at(z, y, 1 - core))

    send_kv(0, 8, at(z + 1, y, core))
    send_kv(0, 16, at(z + 2, y, core))
    for m in range(1, 4):

        @pl.when(y + m < 4)
        def _():
            send_kv(0, 2 * m, at(z, y + m, core))

    @pl.when(core == 0)
    def _():
        to_twin(0)

    def relay_first():
        got_kv(8)
        for m in range(1, 4):
            wrap = (y + m) // 4
            send_kv(8, 2 * (4 + m - 4 * wrap), at(z, y + m, core))
        to_twin(4)

    def relay_second():
        got_kv(16)
        for m in range(1, 4):

            @pl.when(y + m >= 4)
            def _():
                send_kv(16, 2 * (m + 4), at(z, y + m, core))

        @pl.when(core == 1)
        def _():
            to_twin(8)

    def relay_third():
        for d in (1, 2, 3, 5, 6, 7):
            got_kv(2 * d)
            to_twin(d)

    def relay_last():
        for d in range(8):
            got_kv(2 * d + 1)

    for h in range(HEADS_Q):
        base = h * HEAD_WIDTH
        qr[h, :, :128] = (rotate(q[:, base : base + 128].astype(F32), cos, sin) * 1.0).astype(BF16)
        qr[h, :, 128:] = q[:, base + 128 : base + 256]

    first_doc = jnp.where(starts < (me * ROWS).astype(F32), 1.0, 0.0)
    row2 = iota((ROWS, ROWS), 0)
    col2 = iota((ROWS, ROWS), 1)
    same = (seg == seg_row[...]) & (row2 >= col2)
    seg_last = seg[ROWS - 1 : ROWS, :]
    last_doc = jnp.where(seg == seg_last, 1.0, 0.0)
    eye = jnp.where(iota((DK, DK), 0) == iota((DK, DK), 1), 1.0, 0.0)

    def group(g):
        for i in range(PER):
            kh = g * PER + i
            kr = dk[:, lanes(kh, DK)]
            qx = dq[:, lanes(kh, DK)]
            kf = kr.astype(F32)
            qf = qx.astype(F32)
            rk = lax.rsqrt(jnp.sum(kf * kf, axis=1, keepdims=True) + 1e-06)
            rq = lax.rsqrt(jnp.sum(qf * qf, axis=1, keepdims=True) + 1e-06) * DK ** (-0.5)
            rk_row = row_pack[pl.ds(16 + kh, 1), :]
            gram = nt(kr, kr) * (rk * rk_row)
            probe = nt(qx, kr) * (rq * rk_row)
            kn = kf * rk
            qn = qf * rq
            for n in range(2):
                h = 2 * kh + n
                gc = colg[g][:, 2 * i + n : 2 * i + n + 1]
                bc = colb[g][:, 2 * i + n : 2 * i + n + 1]
                gr = row_pack[pl.ds(h, 1), :]
                span = jnp.where(same, jnp.exp(jnp.minimum(gc - gr, 0.0)), 0.0)
                entry = first_doc * jnp.exp(gc)
                solved = inverse((span * gram) * bc)
                vf = pv[:, lanes(h, DK)].astype(F32)
                right = jnp.concatenate([kn * (bc * entry), vf * bc], axis=1).astype(BF16)
                wu = nn(solved, right).astype(BF16)
                inner = nn((span * probe).astype(BF16), wu)
                reach[h] = (qn * entry - inner[:, :DK]).astype(BF16)
                intra[h] = inner[:, DK:]
                tail = last_doc * jnp.exp(jnp.minimum(gc[ROWS - 1 : ROWS] - gc, 0.0))
                both = tn(wu, (kn * tail).astype(BF16))
                mt = eye * entry[ROWS - 1 : ROWS] - both[:DK]
                mta[h] = jnp.concatenate([mt, both[DK:]], axis=0).astype(BF16)

    def send_heads(g):
        @pl.loop(0, 2 * PER)
        def _(i):
            h = g * (2 * PER) + i
            owner = 2 * h

            @pl.when(me != owner)
            def _():
                pltpu.make_async_remote_copy(
                    mta.at[h], inbox.at[lax.rem(me - owner + RANKS, RANKS)], mta_send, mta_recv,
                    device_id={"ctx": owner}, device_id_type=MESH,
                ).start()

            @pl.when(me == owner)
            def _():
                inbox[0] = mta[h]

    @pl.loop(0, GROUPS)
    def _(g):
        group(g)
        send_heads(g)

        @pl.when(g == 0)
        def _():
            relay_first()

        @pl.when(g == 1)
        def _():
            relay_second()

        @pl.when(g == 3)
        def _():
            relay_third()

    relay_last()

    pos0 = iota((ROWS, ROWS), 1).astype(F32)

    def attend(h):
        qh = qr[h]
        best = None
        for j in range(SLOTS):
            s = nt(qh, kv[j, 0])
            pos = pos0 + ((me - j) * ROWS).astype(F32)
            allowed = pos >= starts
            if j == 0:
                allowed = allowed & (row2 >= col2)
            s = jnp.where(allowed, s, NEG)
            s_buf[j] = s
            m2 = jnp.maximum(s[:, :128], s[:, 128:])
            best = m2 if best is None else jnp.maximum(best, m2)
        top = jnp.max(best, axis=1, keepdims=True)
        total = None
        acc = None
        for j in range(SLOTS):
            w = jnp.exp((s_buf[j] - top) * (HEAD_WIDTH ** (-0.5)))
            t2 = w[:, :128] + w[:, 128:]
            total = t2 if total is None else total + t2
            part = nn(w.astype(BF16), kv[j, 1])
            acc = part if acc is None else acc + part
        total = jnp.sum(total, axis=1, keepdims=True)
        gt = gate[:, lanes(h, HEAD_WIDTH)].astype(F32)
        attn_out[:, lanes(h, HEAD_WIDTH)] = (acc / total * jax.nn.sigmoid(gt)).astype(BF16)

    @pl.loop(0, 4)
    def _(h):
        attend(h)

    @pl.when(core == 0)
    def _():
        pltpu.make_async_copy(
            inbox.at[pl.ds(1, RANKS - 1)], inbox.at[pl.ds(1, RANKS - 1)], mta_recv
        ).wait()

        state[...] = jnp.zeros((DK, DK), F32)

        @pl.loop(0, RANKS)
        def _(r):
            j = lax.rem(r - me + RANKS, RANKS)
            stage[j] = state[...].astype(BF16)
            state[...] = nn(stage[j], inbox[j, :DK]) + inbox[j, DK:].astype(F32)

            @pl.when(j != 0)
            def _():
                pltpu.make_async_remote_copy(
                    stage.at[j], state_in.at[chip], st_send, st_recv,
                    device_id={"ctx": r}, device_id_type=MESH,
                ).start()

            @pl.when(j == 0)
            def _():
                state_in[chip] = stage[0]

    @pl.loop(4, HEADS_Q)
    def _(h):
        attend(h)

    @pl.when(core == 0)
    def _():
        pltpu.make_async_copy(state_in.at[pl.ds(0, 15)], state_in.at[pl.ds(0, 15)], st_recv).wait()
        pltpu.make_async_copy(stage.at[pl.ds(1, 31)], stage.at[pl.ds(1, 31)], st_send).wait()
        pltpu.make_async_copy(mta.at[pl.ds(0, 15)], mta.at[pl.ds(0, 15)], mta_send).wait()

    @pl.when(core == 1)
    def _():
        pltpu.make_async_copy(state_in, state_in, st_recv).wait()
        pltpu.make_async_copy(mta, mta, mta_send).wait()

    @pl.loop(0, HEADS_V)
    def _(h):
        out = intra[h] + nt(reach[h], state_in[h])
        spread = lax.rsqrt(jnp.mean(out * out, axis=1, keepdims=True) + 1e-06)
        gt = dgate[:, lanes(h, DK)].astype(F32)
        res = out * spread * gain[...] * (gt * jax.nn.sigmoid(gt))
        delta_out[:, lanes(h, DK)] = res.astype(BF16)

    pltpu.make_async_copy(counts.at[pl.ds(1, 31)], counts.at[pl.ds(1, 31)], cnt_send).wait()

    pltpu.make_async_copy(kv.at[pl.ds(1, 16)], kv.at[pl.ds(1, 16)], kv_send).wait()


def per_device(
    segment_ids, attn_query, attention_keys, attention_values, attn_gate, delta_query, delta_key,
    update_rule_payload, delta_beta, delta_decay, delta_gate, norm_gain,
):
    half = ROTARY_ENTRIES // 2
    index = jnp.arange(half).astype(F32)
    freq = ROPE_THETA ** (-2.0 * index / ROTARY_ENTRIES)
    freq = jnp.concatenate([freq, freq, jnp.zeros((64,), F32)])[None]
    vmem = pl.BlockSpec(memory_space=pltpu.VMEM)
    dma = pltpu.SemaphoreType.DMA
    wide = jax.ShapeDtypeStruct((ROWS, 2048), BF16)
    return pl.pallas_call(
        kernel,
        out_shape=(wide, wide),
        in_specs=[vmem] * 14,
        out_specs=(vmem, vmem),
        scratch_shapes=[
            pltpu.VMEM((8, 128), F32),
            pltpu.VMEM((RANKS, 8, 128), F32),
            pltpu.VMEM((SLOTS, 2, ROWS, HEAD_WIDTH), BF16),
            pltpu.VMEM((GROUPS, ROWS, 2 * PER), F32),
            pltpu.VMEM((GROUPS, ROWS, 2 * PER), F32),
            pltpu.VMEM((128, ROWS), F32),
            pltpu.VMEM((HEADS_V, 2 * DK, DK), BF16),
            pltpu.VMEM((HEADS_V, ROWS, DK), BF16),
            pltpu.VMEM((HEADS_V, ROWS, DK), F32),
            pltpu.VMEM((RANKS, 2 * DK, DK), BF16),
            pltpu.VMEM((RANKS, DK, DK), BF16),
            pltpu.VMEM((HEADS_V, DK, DK), BF16),
            pltpu.VMEM((HEADS_Q, ROWS, HEAD_WIDTH), BF16),
            pltpu.VMEM((SLOTS, ROWS, ROWS), F32),
            pltpu.VMEM((2, ROWS, 128), F32),
            pltpu.VMEM((DK, DK), F32),
            dma, dma, dma, dma((SLOTS,)), dma, dma, dma, dma,
        ],
        compiler_params=pltpu.CompilerParams(
            collective_id=0, has_side_effects=True, vmem_limit_bytes=56 * 2**20
        ),
    )(
        segment_ids.reshape(ROWS, 1), segment_ids.reshape(1, ROWS), freq,
        attn_query, attention_keys, attention_values, attn_gate, delta_query, delta_key,
        update_rule_payload, delta_beta, delta_decay, delta_gate, norm_gain.reshape(1, DK),
    )


def solution(mesh):
    rows = P(("dp", "ctx"))
    wide = P(("dp", "ctx"), None)
    return jax.shard_map(
        per_device,
        mesh=mesh,
        in_specs=(rows,) + (wide,) * 10 + (P(),),
        out_specs=(wide, wide),
        check_vma=False,
    )
```

```python
import jax
import jax.numpy as jnp
import numpy as np
from jax import lax
from jax.experimental import pallas as pl
from jax.experimental.pallas import tpu as pltpu
from jax.sharding import PartitionSpec as P

HEAD_WIDTH = 256
ROTARY_ENTRIES = 64
ROPE_THETA = 10000000.0
DK = 128
DOCS = 8
ROWS = 256
RANKS = 32
SLOTS = 17
HEADS_Q = 8
HEADS_K = 8
HEADS_V = 16
GROUPS = 4
PER = HEADS_K // GROUPS
MESH = pl.DeviceIdType.MESH
F32 = jnp.float32
BF16 = jnp.bfloat16
NEG = -1e30
LOG2E = 1.4426950408889634
CHIPS = 16
KEY, VALUE = 0, 1


def nn(a, b):
    return lax.dot_general(a, b, (((1,), (0,)), ((), ())), preferred_element_type=F32)


def nt(a, b):
    return lax.dot_general(a, b, (((1,), (1,)), ((), ())), preferred_element_type=F32)


def tn(a, b):
    return lax.dot_general(a, b, (((0,), (0,)), ((), ())), preferred_element_type=F32)


def iota(shape, dim):
    return lax.broadcasted_iota(jnp.int32, shape, dim)


def lanes(index, width):
    return pl.ds(pl.multiple_of(index * width, width), width)


def rotate(x, cos, sin):
    lane = iota(x.shape, 1)
    swapped = jnp.where(lane < 32, pltpu.roll(x, 96, 1), pltpu.roll(x, 32, 1))
    return x * cos + swapped * sin


def pair_diag(packed):
    zero = jnp.zeros((128, 128), packed.dtype)
    return jnp.concatenate(
        [
            jnp.concatenate([packed[:, :128], zero], axis=1),
            jnp.concatenate([zero, packed[:, 128:]], axis=1),
        ],
        axis=0,
    )


def inverses(lowers):
    row = iota((128, 256), 0)
    col = iota((128, 256), 1) % 128
    apart = row ^ col
    packed = [jnp.concatenate([x[:128, :128], x[128:, 128:]], axis=1) for x in lowers]
    inv = [jnp.where(apart == 0, 1.0, 0.0) - jnp.where(apart == 1, x, 0.0) for x in packed]
    block = 2
    while block < 128:
        here = (apart >= block) & (apart < 2 * block)
        off = [jnp.where(here, x, 0.0).astype(BF16) for x in packed]
        inv_b = [x.astype(BF16) for x in inv]
        left = [nn(x, pair_diag(c)) for x, c in zip(inv_b, off)]
        inv = [x - nn(c.astype(BF16), pair_diag(b)) for x, c, b in zip(inv, left, inv_b)]
        block *= 2
    inv_b = [x.astype(BF16) for x in inv]
    half = [nn(x[128:, :128].astype(BF16), b[:, :128]) for x, b in zip(lowers, inv_b)]
    corner = [nn(b[:, 128:], c.astype(BF16)) for b, c in zip(inv_b, half)]
    return [
        jnp.concatenate(
            [
                jnp.concatenate([b[:, :128], jnp.zeros((128, 128), BF16)], axis=1),
                jnp.concatenate([(-c).astype(BF16), b[:, 128:]], axis=1),
            ],
            axis=0,
        )
        for b, c in zip(inv_b, corner)
    ]


def kernel(
    seg_row, freq, q, k, v, gate, dq, dk, pv, beta, decay, dgate, gain,
    attn_out, delta_out,
    cnt, counts, kv, colg, colb, row_pack, mta, reach, intra, inbox, stage, state_in,
    qr, s_even, s_odd, top_even, top_odd, bias, state, twin, comb,
    cnt_send, cnt_recv, kv_send, kv_recv, twin_send, twin_recv, comb_send, comb_recv,
    st_send, st_recv, st2_send, st2_recv,
):
    me = lax.axis_index("ctx")
    core = lax.rem(me, 2)
    chip = me // 2
    y = lax.rem(chip, 4)
    z = chip // 4

    def at(zz, yy, cc):
        return {"ctx": (lax.rem(zz, 4) * 4 + lax.rem(yy, 4)) * 2 + cc}

    barrier = pltpu.get_barrier_semaphore()

    @pl.loop(1, RANKS)
    def _(j):
        pl.semaphore_signal(
            barrier, inc=1, device_id={"ctx": lax.rem(me + j, RANKS)}, device_id_type=MESH
        )

    doc = iota((DOCS, ROWS), 0)
    mine = jnp.sum(jnp.where(seg_row[...] == doc, 1.0, 0.0), axis=1, keepdims=True)
    cnt[...] = jnp.broadcast_to(mine, (DOCS, 128))
    counts[0] = jnp.broadcast_to(mine, (DOCS, 128))
    lane1 = iota((ROWS, 128), 1)
    slot = (me * ROWS).astype(F32) + iota((ROWS, 1), 0).astype(F32)
    angle = slot * freq[...]
    cos = jnp.cos(angle)
    sin = jnp.sin(angle) * jnp.where(lane1 < 32, -1.0, 1.0)
    kv[0, KEY, :, :128] = rotate(k[:, :128].astype(F32), cos, sin).astype(BF16)
    kv[0, KEY, :, 128:] = k[:, 128:]
    kv[0, VALUE] = v[...]
    pl.semaphore_wait(barrier, RANKS - 1)

    def send_kv(part, src, dst, target):
        pltpu.make_async_remote_copy(
            kv.at[src, part], kv.at[dst, part], kv_send, kv_recv.at[dst, part],
            device_id=target, device_id_type=MESH,
        ).start()

    def got_kv(part, j):
        pltpu.make_async_copy(kv.at[j, part], kv.at[j, part], kv_recv.at[j, part]).wait()

    def to_twin(part, d):
        send_kv(part, 2 * d, 2 * d + 1 - 2 * core, at(z, y, 1 - core))

    def send_above(part):
        send_kv(part, 0, 8, at(z + 1, y, core))

    def send_own(part):
        for m in (1, 3, 2):

            @pl.when(y + m < 4)
            def _():
                send_kv(part, 0, 2 * m, at(z, y + m, core))

        @pl.when(core == 0)
        def _():
            to_twin(part, 0)

    def slot_of(source, m):
        return 2 * (4 + m - 4 * ((source + m) // 4))

    hop = (3, 1)
    behind = [lax.rem(y + 4 - t, 4) for t in hop]
    passed = [slot_of(b, t) for b, t in zip(behind, hop)]

    def relay_above(part):
        got_kv(part, 8)
        for m in (1, 3):
            send_kv(part, 8, slot_of(y, m), at(z, y + m, core))
        to_twin(part, 4)

    def relay_second(part):
        got_kv(part, 16)
        for m in (3, 1, 2):

            @pl.when(y + m >= 4)
            def _():
                send_kv(part, 16, 2 * (m + 4), at(z, y + m, core))

        @pl.when(core == 1)
        def _():
            to_twin(part, 8)

    def relay_passed(part):
        got_kv(part, passed[part])
        send_kv(part, passed[part], slot_of(behind[part], 2), at(z, y + hop[part], core))
        to_twin(part, passed[part] // 2)

    def relay_rest(part):
        for d in (1, 2, 3, 5, 6, 7):

            @pl.when(passed[part] != 2 * d)
            def _():
                got_kv(part, 2 * d)
                to_twin(part, d)

    def relay_last():
        for d in range(8):
            got_kv(KEY, 2 * d + 1)
            got_kv(VALUE, 2 * d + 1)

    @pl.loop(1, RANKS)
    def _(j):
        pltpu.make_async_remote_copy(
            cnt, counts.at[j], cnt_send, cnt_recv.at[jnp.minimum(j - 1, 1)],
            device_id={"ctx": lax.rem(me + j, RANKS)}, device_id_type=MESH,
        ).start()

    send_above(VALUE)
    send_above(KEY)
    send_own(VALUE)
    send_own(KEY)
    sums_of = jnp.where(iota((ROWS, ROWS), 0) <= iota((ROWS, ROWS), 1), 1.0, 0.0).astype(BF16)
    dec = decay[...]
    hi = dec.astype(BF16)
    mid = (dec - hi.astype(F32)).astype(BF16)
    low = (dec - hi.astype(F32) - mid.astype(F32)).astype(BF16)
    sums = nn(hi, sums_of) + nn(mid, sums_of) + nn(low, sums_of)
    row_pack[...] = sums
    seg_f = seg_row[...].astype(F32)
    pack = jnp.concatenate(
        [
            sums, beta[...],
            jnp.broadcast_to(seg_f, (96, ROWS)),
        ],
        axis=0,
    )
    columns = pack.T
    seg = columns[:, 32:33].astype(jnp.int32)
    for g in range(GROUPS):
        w = 2 * PER
        colg[g, :, :w] = columns[:, g * w : (g + 1) * w]
        colb[g, :, :w] = columns[:, 16 + g * w : 16 + (g + 1) * w]

    relay_above(VALUE)
    send_kv(VALUE, 0, 16, at(z + 2, y, core))
    send_kv(KEY, 0, 16, at(z + 2, y, core))

    for h in range(HEADS_Q):
        base = h * HEAD_WIDTH
        qr[h, :, :128] = rotate(q[:, base : base + 128].astype(F32), cos, sin).astype(BF16)
        qr[h, :, 128:] = q[:, base + 128 : base + 256]

    pltpu.make_async_copy(counts.at[1], counts.at[1], cnt_recv.at[0]).wait()
    held = jnp.where(counts[1] > 0.0, iota((DOCS, 128), 0).astype(F32), -1.0)
    held = jnp.where(me > 0, jnp.max(held, axis=0, keepdims=True), -1.0)
    first_doc = jnp.where(seg.astype(F32) == held[:, :1], 1.0, 0.0)
    row2 = iota((ROWS, ROWS), 0)
    col2 = iota((ROWS, ROWS), 1)
    same = (seg == seg_row[...]) & (row2 >= col2)
    seg_last = seg[ROWS - 1 : ROWS, :]
    last_doc = jnp.where(seg == seg_last, 1.0, 0.0)
    eye = jnp.where(iota((DK, DK), 0) == iota((DK, DK), 1), 1.0, 0.0)

    relay_above(KEY)

    def group(g):
        parts = []
        for i in range(PER):
            kh = g * PER + i
            kr = dk[:, lanes(kh, DK)]
            qx = dq[:, lanes(kh, DK)]
            kf = kr.astype(F32)
            qf = qx.astype(F32)
            rk = lax.rsqrt(jnp.sum(kf * kf, axis=1, keepdims=True) + 1e-06)
            rq = lax.rsqrt(jnp.sum(qf * qf, axis=1, keepdims=True) + 1e-06) * DK ** (-0.5)
            rk_row = jnp.broadcast_to(rk, (ROWS, 128)).T[0:1]
            gram = nt(kr, kr) * (rk * rk_row)
            probe = nt(qx, kr) * (rq * rk_row)
            for n in range(2):
                gc = colg[g][:, 2 * i + n : 2 * i + n + 1]
                bc = colb[g][:, 2 * i + n : 2 * i + n + 1]
                gr = row_pack[pl.ds(2 * kh + n, 1), :]
                span = jnp.where(same, jnp.exp(jnp.minimum(gc - gr, 0.0)), 0.0)
                parts.append((2 * kh + n, kf * rk, qf * rq, gc, bc, (span * gram) * bc, (span * probe).astype(BF16)))
        solved = inverses([p[5] for p in parts])

        @pl.when(g == 0)
        def _():
            relay_passed(VALUE)

        @pl.when(g == 1)
        def _():
            relay_passed(KEY)

        wus = []
        for (h, kn, qn, gc, bc, _, _), inv in zip(parts, solved):
            entry = first_doc * jnp.exp(gc)
            vf = pv[:, lanes(h, DK)].astype(F32)
            right = jnp.concatenate([kn * (bc * entry), vf * bc], axis=1).astype(BF16)
            wus.append(nn(inv, right).astype(BF16))
        inners = [nn(p[6], wu) for p, wu in zip(parts, wus)]
        boths = []
        for (h, kn, qn, gc, bc, _, _), wu in zip(parts, wus):
            tail = last_doc * jnp.exp(jnp.minimum(gc[ROWS - 1 : ROWS] - gc, 0.0))
            boths.append(tn(wu, (kn * tail).astype(BF16)))
        for (h, kn, qn, gc, bc, _, _), inner, both in zip(parts, inners, boths):
            entry = first_doc * jnp.exp(gc)
            reach[h] = (qn * entry - inner[:, :DK]).astype(BF16)
            intra[h] = inner[:, DK:]
            mt = eye * entry[ROWS - 1 : ROWS] - both[:DK]
            mta[h] = jnp.concatenate([mt, both[DK:]], axis=0).astype(BF16)

    heads = 2 * PER

    def send_heads(g):
        @pl.when(core == 0)
        def _():
            pltpu.make_async_remote_copy(
                mta.at[pl.ds(g * heads, heads)], twin.at[pl.ds(g * heads, heads)],
                twin_send, twin_recv.at[g],
                device_id={"ctx": me + 1}, device_id_type=MESH,
            ).start()

        @pl.when(core == 1)
        def _():
            pltpu.make_async_copy(
                twin.at[pl.ds(g * heads, heads)], twin.at[pl.ds(g * heads, heads)], twin_recv.at[g]
            ).wait()

            @pl.loop(0, heads)
            def _(i):
                h = g * heads + i
                both = nn(twin[h], mta[h, :DK])
                comb[h, :DK] = both[:DK].astype(BF16)
                comb[h, DK:] = (both[DK:] + mta[h, DK:].astype(F32)).astype(BF16)

    @pl.loop(0, GROUPS)
    def _(g):
        group(g)

        @pl.when(g == 0)
        def _():
            relay_second(VALUE)

        @pl.when(g == 1)
        def _():
            relay_second(KEY)

        @pl.when(g == 2)
        def _():
            relay_rest(VALUE)

        @pl.when(g == 3)
        def _():
            relay_rest(KEY)

        send_heads(g)

    relay_last()

    @pl.when(core == 1)
    def _():
        @pl.loop(0, HEADS_V)
        def _(i):
            h = lax.rem(chip + i, CHIPS)
            pltpu.make_async_remote_copy(
                comb.at[h], inbox.at[lax.rem(CHIPS - i, CHIPS)], comb_send, comb_recv,
                device_id={"ctx": 2 * h}, device_id_type=MESH,
            ).start()

    pltpu.make_async_copy(
        counts.at[pl.ds(2, RANKS - 2)], counts.at[pl.ds(2, RANKS - 2)], cnt_recv.at[1]
    ).wait()
    totals = jnp.sum(counts[...], axis=0)
    totals = jnp.concatenate([totals, totals], axis=1)
    start_row = jnp.sum(jnp.where(doc < seg_row[...], totals, 0.0), axis=0, keepdims=True)
    starts = jnp.broadcast_to(start_row, (128, ROWS)).T[:, :1]
    pos0 = iota((ROWS, ROWS), 1).astype(F32)
    for j in range(SLOTS):
        allowed = (pos0 + ((me - j) * ROWS).astype(F32)) >= starts
        if j == 0:
            allowed = allowed & (row2 >= col2)
        bias[j] = jnp.where(allowed, 0.0, NEG)

    def overlap(low, now, now_top, later, later_top):
        nxt = jnp.minimum(low + 1, HEADS_Q - 1)
        best = total = acc = None
        if now is not None:
            top = now_top[...]
            top = jnp.concatenate([top, top], axis=1)
        for j in range(SLOTS):
            if later is not None:
                s = nt(qr[nxt], kv[j, 0]) + bias[j]
                later[j] = s
                m2 = jnp.maximum(s[:, :128], s[:, 128:])
                best = m2 if best is None else jnp.maximum(best, m2)
            if now is not None:
                w = jnp.exp2((now[j] - top) * (LOG2E * HEAD_WIDTH ** (-0.5)))
                t2 = w[:, :128] + w[:, 128:]
                total = t2 if total is None else total + t2
                part = nn(w.astype(BF16), kv[j, 1])
                acc = part if acc is None else acc + part
        if later is not None:
            later_top[...] = jnp.broadcast_to(jnp.max(best, axis=1, keepdims=True), (ROWS, 128))
        if now is not None:
            total = jnp.sum(total, axis=1, keepdims=True)
            gt = gate[:, lanes(low, HEAD_WIDTH)].astype(F32)
            attn_out[:, lanes(low, HEAD_WIDTH)] = (
                acc * (1.0 / total) * jax.nn.sigmoid(gt)
            ).astype(BF16)

    def two_heads(i):
        overlap(2 * i, s_even, top_even, s_odd, top_odd)
        overlap(2 * i + 1, s_odd, top_odd, s_even, top_even)

    overlap(-1, None, None, s_even, top_even)

    @pl.loop(0, 4)
    def _(i):
        two_heads(i)

        @pl.when((core == 0) & (i == 2))
        def _():
            pltpu.make_async_copy(inbox, inbox, comb_recv).wait()
            state[...] = jnp.zeros((DK, DK), F32)

            @pl.loop(0, CHIPS)
            def _(c):
                j = lax.rem(c - chip + CHIPS, CHIPS)
                stage[j] = state[...].astype(BF16)
                state[...] = nn(stage[j], inbox[j, :DK]) + inbox[j, DK:].astype(F32)

                @pl.when(j != 0)
                def _():
                    pltpu.make_async_remote_copy(
                        stage.at[j], state_in.at[chip], st_send, st_recv,
                        device_id={"ctx": 2 * c}, device_id_type=MESH,
                    ).start()

                @pl.when(j == 0)
                def _():
                    state_in[chip] = stage[0]

        @pl.when((core == 0) & (i == 3))
        def _():
            pltpu.make_async_copy(state_in.at[pl.ds(0, 15)], state_in.at[pl.ds(0, 15)], st_recv).wait()
            pltpu.make_async_remote_copy(
                state_in, state_in, st2_send, st2_recv,
                device_id={"ctx": me + 1}, device_id_type=MESH,
            ).start()

    @pl.when(core == 1)
    def _():
        pltpu.make_async_copy(state_in, state_in, st2_recv).wait()

        @pl.loop(0, HEADS_V)
        def _(h):
            state_in[h] = (
                nn(state_in[h], twin[h, :DK]) + twin[h, DK:].astype(F32)
            ).astype(BF16)

        pltpu.make_async_copy(comb, comb, comb_send).wait()

    @pl.loop(0, HEADS_V // 4)
    def _(t):
        for i in range(4):
            h = 4 * t + i
            out = intra[h] + nt(reach[h], state_in[h])
            spread = lax.rsqrt(jnp.mean(out * out, axis=1, keepdims=True) + 1e-06)
            gt = dgate[:, lanes(h, DK)].astype(F32)
            res = out * spread * gain[...] * (gt * jax.nn.sigmoid(gt))
            delta_out[:, lanes(h, DK)] = res.astype(BF16)

    @pl.when(core == 0)
    def _():
        pltpu.make_async_copy(mta, mta, twin_send).wait()
        pltpu.make_async_copy(stage.at[pl.ds(1, 15)], stage.at[pl.ds(1, 15)], st_send).wait()
        pltpu.make_async_copy(state_in, state_in, st2_send).wait()

    pltpu.make_async_copy(counts.at[pl.ds(1, 31)], counts.at[pl.ds(1, 31)], cnt_send).wait()

    pltpu.make_async_copy(kv.at[pl.ds(1, 16)], kv.at[pl.ds(1, 16)], kv_send).wait()


def per_device(
    segment_ids, attn_query, attention_keys, attention_values, attn_gate, delta_query, delta_key,
    update_rule_payload, delta_beta, delta_decay, delta_gate, norm_gain,
):
    entry = np.arange(128)
    freq = np.where(
        entry < ROTARY_ENTRIES, ROPE_THETA ** (-2.0 * (entry % 32) / ROTARY_ENTRIES), 0.0
    ).astype(np.float32)[None]
    vmem = pl.BlockSpec(memory_space=pltpu.VMEM)
    dma = pltpu.SemaphoreType.DMA
    wide = jax.ShapeDtypeStruct((ROWS, 2048), BF16)
    return pl.pallas_call(
        kernel,
        out_shape=(wide, wide),
        in_specs=[vmem] * 13,
        out_specs=(vmem, vmem),
        scratch_shapes=[
            pltpu.VMEM((8, 128), F32),
            pltpu.VMEM((RANKS, 8, 128), F32),
            pltpu.VMEM((SLOTS, 2, ROWS, HEAD_WIDTH), BF16),
            pltpu.VMEM((GROUPS, ROWS, 2 * PER), F32),
            pltpu.VMEM((GROUPS, ROWS, 2 * PER), F32),
            pltpu.VMEM((HEADS_V, ROWS), F32),
            pltpu.VMEM((HEADS_V, 2 * DK, DK), BF16),
            pltpu.VMEM((HEADS_V, ROWS, DK), BF16),
            pltpu.VMEM((HEADS_V, ROWS, DK), F32),
            pltpu.VMEM((CHIPS, 2 * DK, DK), BF16),
            pltpu.VMEM((CHIPS, DK, DK), BF16),
            pltpu.VMEM((HEADS_V, DK, DK), BF16),
            pltpu.VMEM((HEADS_Q, ROWS, HEAD_WIDTH), BF16),
            pltpu.VMEM((SLOTS, ROWS, ROWS), F32),
            pltpu.VMEM((SLOTS, ROWS, ROWS), F32),
            pltpu.VMEM((ROWS, 128), F32),
            pltpu.VMEM((ROWS, 128), F32),
            pltpu.VMEM((SLOTS, ROWS, ROWS), F32),
            pltpu.VMEM((DK, DK), F32),
            pltpu.VMEM((HEADS_V, 2 * DK, DK), BF16),
            pltpu.VMEM((HEADS_V, 2 * DK, DK), BF16),
            dma, dma((2,)), dma, dma((SLOTS, 2)), dma, dma((GROUPS,)), dma, dma, dma, dma, dma, dma,
        ],
        compiler_params=pltpu.CompilerParams(
            collective_id=0, has_side_effects=True, vmem_limit_bytes=56 * 2**20
        ),
    )(
        segment_ids.reshape(1, ROWS), freq,
        attn_query, attention_keys, attention_values, attn_gate, delta_query, delta_key,
        update_rule_payload, delta_beta.T, delta_decay.T, delta_gate, norm_gain.reshape(1, DK),
    )


def solution(mesh):
    rows = P(("dp", "ctx"))
    wide = P(("dp", "ctx"), None)
    return jax.shard_map(
        per_device,
        mesh=mesh,
        in_specs=(rows,) + (wide,) * 10 + (P(),),
        out_specs=(wide, wide),
        check_vma=False,
    )
```

```python
import jax
import jax.numpy as jnp
import numpy as np
from jax import lax
from jax.experimental import pallas as pl
from jax.experimental.pallas import tpu as pltpu
from jax.sharding import PartitionSpec as P

HEAD_WIDTH = 256
ROTARY_ENTRIES = 64
ROPE_THETA = 10000000.0
DK = 128
DOCS = 8
ROWS = 256
RANKS = 32
SLOTS = 17
HEADS_Q = 8
HEADS_K = 8
HEADS_V = 16
GROUPS = 4
PER = HEADS_K // GROUPS
MESH = pl.DeviceIdType.MESH
F32 = jnp.float32
BF16 = jnp.bfloat16
NEG = -1e30
LOG2E = 1.4426950408889634
CHIPS = 16
KEY, VALUE = 0, 1


def nn(a, b):
    return lax.dot_general(a, b, (((1,), (0,)), ((), ())), preferred_element_type=F32)


def nt(a, b):
    return lax.dot_general(a, b, (((1,), (1,)), ((), ())), preferred_element_type=F32)


def tn(a, b):
    return lax.dot_general(a, b, (((0,), (0,)), ((), ())), preferred_element_type=F32)


def iota(shape, dim):
    return lax.broadcasted_iota(jnp.int32, shape, dim)


def lanes(index, width):
    return pl.ds(pl.multiple_of(index * width, width), width)


def rotate(x, cos, sin):
    lane = iota(x.shape, 1)
    swapped = jnp.where(lane < 32, pltpu.roll(x, 96, 1), pltpu.roll(x, 32, 1))
    return x * cos + swapped * sin


def pair_diag(packed):
    zero = jnp.zeros((128, 128), packed.dtype)
    return jnp.concatenate(
        [
            jnp.concatenate([packed[:, :128], zero], axis=1),
            jnp.concatenate([zero, packed[:, 128:]], axis=1),
        ],
        axis=0,
    )


def inverses(lowers):
    row = iota((128, 256), 0)
    col = iota((128, 256), 1) % 128
    apart = row ^ col
    packed = [jnp.concatenate([x[:128, :128], x[128:, 128:]], axis=1) for x in lowers]
    inv = [jnp.where(apart == 0, 1.0, 0.0) - jnp.where(apart == 1, x, 0.0) for x in packed]
    block = 2
    while block < 128:
        here = (apart >= block) & (apart < 2 * block)
        off = [jnp.where(here, x, 0.0).astype(BF16) for x in packed]
        inv_b = [x.astype(BF16) for x in inv]
        left = [nn(x, pair_diag(c)) for x, c in zip(inv_b, off)]
        inv = [x - nn(c.astype(BF16), pair_diag(b)) for x, c, b in zip(inv, left, inv_b)]
        block *= 2
    inv_b = [x.astype(BF16) for x in inv]
    half = [nn(x[128:, :128].astype(BF16), b[:, :128]) for x, b in zip(lowers, inv_b)]
    corner = [nn(b[:, 128:], c.astype(BF16)) for b, c in zip(inv_b, half)]
    return [
        jnp.concatenate(
            [
                jnp.concatenate([b[:, :128], jnp.zeros((128, 128), BF16)], axis=1),
                jnp.concatenate([(-c).astype(BF16), b[:, 128:]], axis=1),
            ],
            axis=0,
        )
        for b, c in zip(inv_b, corner)
    ]


def kernel(
    seg_row, freq, q_hbm, k, v, gate_hbm, dq_hbm, dk_hbm, pv_hbm, beta, decay, dgate_hbm, gain,
    attn_out, delta_out,
    cnt, counts, kv, colg, colb, row_pack, mta, reach, intra, inbox, stage, state_in,
    qr, s_even, s_odd, top_even, top_odd, bias, state, twin, comb,
    cnt_send, cnt_recv, kv_send, kv_recv, twin_send, twin_recv, comb_send, comb_recv,
    st_send, st_recv, st2_send, st2_recv,
    q, gate, dq, dk, pv, dgate, in_sem,
):
    me = lax.axis_index("ctx")
    core = lax.rem(me, 2)
    chip = me // 2
    y = lax.rem(chip, 4)
    z = chip // 4

    def at(zz, yy, cc):
        return {"ctx": (lax.rem(zz, 4) * 4 + lax.rem(yy, 4)) * 2 + cc}

    barrier = pltpu.get_barrier_semaphore()

    @pl.loop(1, RANKS)
    def _(j):
        pl.semaphore_signal(
            barrier, inc=1, device_id={"ctx": lax.rem(me + j, RANKS)}, device_id_type=MESH
        )

    loads = [
        pltpu.make_async_copy(src, dst, in_sem.at[n])
        for n, (src, dst) in enumerate(
            [(q_hbm, q), (dq_hbm, dq), (dk_hbm, dk), (pv_hbm, pv), (gate_hbm, gate), (dgate_hbm, dgate)]
        )
    ]
    for load in loads:
        load.start()

    doc = iota((DOCS, ROWS), 0)
    mine = jnp.sum(jnp.where(seg_row[...] == doc, 1.0, 0.0), axis=1, keepdims=True)
    cnt[...] = jnp.broadcast_to(mine, (DOCS, 128))
    counts[0] = jnp.broadcast_to(mine, (DOCS, 128))
    lane1 = iota((ROWS, 128), 1)
    slot = (me * ROWS).astype(F32) + iota((ROWS, 1), 0).astype(F32)
    angle = slot * freq[...]
    cos = jnp.cos(angle)
    sin = jnp.sin(angle) * jnp.where(lane1 < 32, -1.0, 1.0)
    kv[0, KEY, :, :128] = rotate(k[:, :128].astype(F32), cos, sin).astype(BF16)
    kv[0, KEY, :, 128:] = k[:, 128:]
    kv[0, VALUE] = v[...]
    pl.semaphore_wait(barrier, RANKS - 1)

    def send_kv(part, src, dst, target):
        pltpu.make_async_remote_copy(
            kv.at[src, part], kv.at[dst, part], kv_send, kv_recv.at[dst, part],
            device_id=target, device_id_type=MESH,
        ).start()

    def got_kv(part, j):
        pltpu.make_async_copy(kv.at[j, part], kv.at[j, part], kv_recv.at[j, part]).wait()

    def to_twin(part, d):
        send_kv(part, 2 * d, 2 * d + 1 - 2 * core, at(z, y, 1 - core))

    def send_above(part):
        send_kv(part, 0, 8, at(z + 1, y, core))

    def send_own(part):
        for m in (1, 3, 2):

            @pl.when(y + m < 4)
            def _():
                send_kv(part, 0, 2 * m, at(z, y + m, core))

        @pl.when(core == 0)
        def _():
            to_twin(part, 0)

    def slot_of(source, m):
        return 2 * (4 + m - 4 * ((source + m) // 4))

    hop = (3, 1)
    behind = [lax.rem(y + 4 - t, 4) for t in hop]
    passed = [slot_of(b, t) for b, t in zip(behind, hop)]

    def relay_above(part):
        got_kv(part, 8)
        for m in (1, 3):
            send_kv(part, 8, slot_of(y, m), at(z, y + m, core))
        to_twin(part, 4)

    def relay_second(part):
        got_kv(part, 16)
        for m in (3, 1, 2):

            @pl.when(y + m >= 4)
            def _():
                send_kv(part, 16, 2 * (m + 4), at(z, y + m, core))

        @pl.when(core == 1)
        def _():
            to_twin(part, 8)

    def relay_passed(part):
        got_kv(part, passed[part])
        send_kv(part, passed[part], slot_of(behind[part], 2), at(z, y + hop[part], core))
        to_twin(part, passed[part] // 2)

    def relay_rest(part):
        for d in (1, 2, 3, 5, 6, 7):

            @pl.when(passed[part] != 2 * d)
            def _():
                got_kv(part, 2 * d)
                to_twin(part, d)

    def relay_last():
        for d in range(8):
            got_kv(KEY, 2 * d + 1)
            got_kv(VALUE, 2 * d + 1)

    @pl.loop(1, RANKS)
    def _(j):
        pltpu.make_async_remote_copy(
            cnt, counts.at[j], cnt_send, cnt_recv.at[jnp.minimum(j - 1, 1)],
            device_id={"ctx": lax.rem(me + j, RANKS)}, device_id_type=MESH,
        ).start()

    send_above(VALUE)
    send_above(KEY)
    send_own(VALUE)
    send_own(KEY)
    sums_of = jnp.where(iota((ROWS, ROWS), 0) <= iota((ROWS, ROWS), 1), 1.0, 0.0).astype(BF16)
    dec = decay[...]
    hi = dec.astype(BF16)
    mid = (dec - hi.astype(F32)).astype(BF16)
    low = (dec - hi.astype(F32) - mid.astype(F32)).astype(BF16)
    sums = nn(hi, sums_of) + nn(mid, sums_of) + nn(low, sums_of)
    row_pack[...] = sums
    seg_f = seg_row[...].astype(F32)
    pack = jnp.concatenate(
        [
            sums, beta[...],
            jnp.broadcast_to(seg_f, (96, ROWS)),
        ],
        axis=0,
    )
    columns = pack.T
    seg = columns[:, 32:33].astype(jnp.int32)
    for g in range(GROUPS):
        w = 2 * PER
        colg[g, :, :w] = columns[:, g * w : (g + 1) * w]
        colb[g, :, :w] = columns[:, 16 + g * w : 16 + (g + 1) * w]

    relay_above(VALUE)
    send_kv(VALUE, 0, 16, at(z + 2, y, core))
    send_kv(KEY, 0, 16, at(z + 2, y, core))

    loads[0].wait()
    for h in range(HEADS_Q):
        base = h * HEAD_WIDTH
        qr[h, :, :128] = rotate(q[:, base : base + 128].astype(F32), cos, sin).astype(BF16)
        qr[h, :, 128:] = q[:, base + 128 : base + 256]

    pltpu.make_async_copy(counts.at[1], counts.at[1], cnt_recv.at[0]).wait()
    held = jnp.where(counts[1] > 0.0, iota((DOCS, 128), 0).astype(F32), -1.0)
    held = jnp.where(me > 0, jnp.max(held, axis=0, keepdims=True), -1.0)
    first_doc = jnp.where(seg.astype(F32) == held[:, :1], 1.0, 0.0)
    row2 = iota((ROWS, ROWS), 0)
    col2 = iota((ROWS, ROWS), 1)
    same = (seg == seg_row[...]) & (row2 >= col2)
    seg_last = seg[ROWS - 1 : ROWS, :]
    last_doc = jnp.where(seg == seg_last, 1.0, 0.0)
    eye = jnp.where(iota((DK, DK), 0) == iota((DK, DK), 1), 1.0, 0.0)

    relay_above(KEY)

    def group(g):
        parts = []
        for i in range(PER):
            kh = g * PER + i
            kr = dk[:, lanes(kh, DK)]
            qx = dq[:, lanes(kh, DK)]
            kf = kr.astype(F32)
            qf = qx.astype(F32)
            rk = lax.rsqrt(jnp.sum(kf * kf, axis=1, keepdims=True) + 1e-06)
            rq = lax.rsqrt(jnp.sum(qf * qf, axis=1, keepdims=True) + 1e-06) * DK ** (-0.5)
            rk_row = jnp.broadcast_to(rk, (ROWS, 128)).T[0:1]
            gram = nt(kr, kr) * (rk * rk_row)
            probe = nt(qx, kr) * (rq * rk_row)
            for n in range(2):
                gc = colg[g][:, 2 * i + n : 2 * i + n + 1]
                bc = colb[g][:, 2 * i + n : 2 * i + n + 1]
                gr = row_pack[pl.ds(2 * kh + n, 1), :]
                span = jnp.where(same, jnp.exp(jnp.minimum(gc - gr, 0.0)), 0.0)
                parts.append((2 * kh + n, kf * rk, qf * rq, gc, bc, (span * gram) * bc, (span * probe).astype(BF16)))
        solved = inverses([p[5] for p in parts])

        @pl.when(g == 0)
        def _():
            relay_passed(VALUE)

        @pl.when(g == 1)
        def _():
            relay_passed(KEY)

        wus = []
        for (h, kn, qn, gc, bc, _, _), inv in zip(parts, solved):
            entry = first_doc * jnp.exp(gc)
            vf = pv[:, lanes(h, DK)].astype(F32)
            right = jnp.concatenate([kn * (bc * entry), vf * bc], axis=1).astype(BF16)
            wus.append(nn(inv, right).astype(BF16))
        inners = [nn(p[6], wu) for p, wu in zip(parts, wus)]
        boths = []
        for (h, kn, qn, gc, bc, _, _), wu in zip(parts, wus):
            tail = last_doc * jnp.exp(jnp.minimum(gc[ROWS - 1 : ROWS] - gc, 0.0))
            boths.append(tn(wu, (kn * tail).astype(BF16)))
        for (h, kn, qn, gc, bc, _, _), inner, both in zip(parts, inners, boths):
            entry = first_doc * jnp.exp(gc)
            reach[h] = (qn * entry - inner[:, :DK]).astype(BF16)
            intra[h] = inner[:, DK:]
            mt = eye * entry[ROWS - 1 : ROWS] - both[:DK]
            mta[h] = jnp.concatenate([mt, both[DK:]], axis=0).astype(BF16)

    heads = 2 * PER

    def send_heads(g):
        @pl.when(core == 0)
        def _():
            pltpu.make_async_remote_copy(
                mta.at[pl.ds(g * heads, heads)], twin.at[pl.ds(g * heads, heads)],
                twin_send, twin_recv.at[g],
                device_id={"ctx": me + 1}, device_id_type=MESH,
            ).start()

        @pl.when(core == 1)
        def _():
            pltpu.make_async_copy(
                twin.at[pl.ds(g * heads, heads)], twin.at[pl.ds(g * heads, heads)], twin_recv.at[g]
            ).wait()

            @pl.loop(0, heads)
            def _(i):
                h = g * heads + i
                both = nn(twin[h], mta[h, :DK])
                comb[h, :DK] = both[:DK].astype(BF16)
                comb[h, DK:] = (both[DK:] + mta[h, DK:].astype(F32)).astype(BF16)
                pltpu.make_async_remote_copy(
                    comb.at[h], inbox.at[lax.rem(chip - h + CHIPS, CHIPS)], comb_send, comb_recv,
                    device_id={"ctx": 2 * h}, device_id_type=MESH,
                ).start()

    for load in loads[1:4]:
        load.wait()

    @pl.loop(0, GROUPS)
    def _(g):
        group(g)

        @pl.when(g == 0)
        def _():
            relay_second(VALUE)

        @pl.when(g == 1)
        def _():
            relay_second(KEY)

        @pl.when(g == 2)
        def _():
            relay_rest(VALUE)

        @pl.when(g == 3)
        def _():
            relay_rest(KEY)

        send_heads(g)

    relay_last()

    pltpu.make_async_copy(
        counts.at[pl.ds(2, RANKS - 2)], counts.at[pl.ds(2, RANKS - 2)], cnt_recv.at[1]
    ).wait()
    totals = jnp.sum(counts[...], axis=0)
    totals = jnp.concatenate([totals, totals], axis=1)
    start_row = jnp.sum(jnp.where(doc < seg_row[...], totals, 0.0), axis=0, keepdims=True)
    starts = jnp.broadcast_to(start_row, (128, ROWS)).T[:, :1]
    pos0 = iota((ROWS, ROWS), 1).astype(F32)
    for j in range(SLOTS):
        allowed = (pos0 + ((me - j) * ROWS).astype(F32)) >= starts
        if j == 0:
            allowed = allowed & (row2 >= col2)
        bias[j] = jnp.where(allowed, 0.0, NEG)

    def overlap(low, now, now_top, later, later_top):
        nxt = jnp.minimum(low + 1, HEADS_Q - 1)
        best = total = acc = None
        if now is not None:
            top = now_top[...]
            top = jnp.concatenate([top, top], axis=1)
        for j in range(SLOTS):
            if later is not None:
                s = nt(qr[nxt], kv[j, 0]) + bias[j]
                later[j] = s
                m2 = jnp.maximum(s[:, :128], s[:, 128:])
                best = m2 if best is None else jnp.maximum(best, m2)
            if now is not None:
                w = jnp.exp2((now[j] - top) * (LOG2E * HEAD_WIDTH ** (-0.5)))
                t2 = w[:, :128] + w[:, 128:]
                total = t2 if total is None else total + t2
                part = nn(w.astype(BF16), kv[j, 1])
                acc = part if acc is None else acc + part
        if later is not None:
            later_top[...] = jnp.broadcast_to(jnp.max(best, axis=1, keepdims=True), (ROWS, 128))
        if now is not None:
            total = jnp.sum(total, axis=1, keepdims=True)
            gt = gate[:, lanes(low, HEAD_WIDTH)].astype(F32)
            attn_out[:, lanes(low, HEAD_WIDTH)] = (
                acc * (1.0 / total) * jax.nn.sigmoid(gt)
            ).astype(BF16)

    def two_heads(i):
        overlap(2 * i, s_even, top_even, s_odd, top_odd)
        overlap(2 * i + 1, s_odd, top_odd, s_even, top_even)

    overlap(-1, None, None, s_even, top_even)
    loads[4].wait()
    loads[5].wait()

    @pl.loop(0, 4)
    def _(i):
        two_heads(i)

        @pl.when((core == 0) & (i == 1))
        def _():
            pltpu.make_async_copy(inbox, inbox, comb_recv).wait()
            state[...] = jnp.zeros((DK, DK), F32)

            @pl.loop(0, CHIPS)
            def _(c):
                j = lax.rem(c - chip + CHIPS, CHIPS)
                stage[j] = state[...].astype(BF16)
                state[...] = nn(stage[j], inbox[j, :DK]) + inbox[j, DK:].astype(F32)

                @pl.when(j != 0)
                def _():
                    pltpu.make_async_remote_copy(
                        stage.at[j], state_in.at[chip], st_send, st_recv,
                        device_id={"ctx": 2 * c}, device_id_type=MESH,
                    ).start()

                @pl.when(j == 0)
                def _():
                    state_in[chip] = stage[0]

        @pl.when((core == 0) & (i == 2))
        def _():
            pltpu.make_async_copy(state_in.at[pl.ds(0, 15)], state_in.at[pl.ds(0, 15)], st_recv).wait()
            pltpu.make_async_remote_copy(
                state_in, state_in, st2_send, st2_recv,
                device_id={"ctx": me + 1}, device_id_type=MESH,
            ).start()

    @pl.when(core == 1)
    def _():
        pltpu.make_async_copy(state_in, state_in, st2_recv).wait()

        @pl.loop(0, HEADS_V)
        def _(h):
            state_in[h] = (
                nn(state_in[h], twin[h, :DK]) + twin[h, DK:].astype(F32)
            ).astype(BF16)

        pltpu.make_async_copy(comb, comb, comb_send).wait()

    @pl.loop(0, HEADS_V // 4)
    def _(t):
        for i in range(4):
            h = 4 * t + i
            out = intra[h] + nt(reach[h], state_in[h])
            spread = lax.rsqrt(jnp.mean(out * out, axis=1, keepdims=True) + 1e-06)
            gt = dgate[:, lanes(h, DK)].astype(F32)
            res = out * spread * gain[...] * (gt * jax.nn.sigmoid(gt))
            delta_out[:, lanes(h, DK)] = res.astype(BF16)

    @pl.when(core == 0)
    def _():
        pltpu.make_async_copy(mta, mta, twin_send).wait()
        pltpu.make_async_copy(stage.at[pl.ds(1, 15)], stage.at[pl.ds(1, 15)], st_send).wait()
        pltpu.make_async_copy(state_in, state_in, st2_send).wait()

    pltpu.make_async_copy(counts.at[pl.ds(1, 31)], counts.at[pl.ds(1, 31)], cnt_send).wait()

    pltpu.make_async_copy(kv.at[pl.ds(1, 16)], kv.at[pl.ds(1, 16)], kv_send).wait()


def per_device(
    segment_ids, attn_query, attention_keys, attention_values, attn_gate, delta_query, delta_key,
    update_rule_payload, delta_beta, delta_decay, delta_gate, norm_gain,
):
    entry = np.arange(128)
    freq = np.where(
        entry < ROTARY_ENTRIES, ROPE_THETA ** (-2.0 * (entry % 32) / ROTARY_ENTRIES), 0.0
    ).astype(np.float32)[None]
    vmem = pl.BlockSpec(memory_space=pltpu.VMEM)
    hbm = pl.BlockSpec(memory_space=pl.ANY)
    dma = pltpu.SemaphoreType.DMA
    wide = jax.ShapeDtypeStruct((ROWS, 2048), BF16)
    return pl.pallas_call(
        kernel,
        out_shape=(wide, wide),
        in_specs=[vmem, vmem, hbm, vmem, vmem, hbm, hbm, hbm, hbm, vmem, vmem, hbm, vmem],
        out_specs=(vmem, vmem),
        scratch_shapes=[
            pltpu.VMEM((8, 128), F32),
            pltpu.VMEM((RANKS, 8, 128), F32),
            pltpu.VMEM((SLOTS, 2, ROWS, HEAD_WIDTH), BF16),
            pltpu.VMEM((GROUPS, ROWS, 2 * PER), F32),
            pltpu.VMEM((GROUPS, ROWS, 2 * PER), F32),
            pltpu.VMEM((HEADS_V, ROWS), F32),
            pltpu.VMEM((HEADS_V, 2 * DK, DK), BF16),
            pltpu.VMEM((HEADS_V, ROWS, DK), BF16),
            pltpu.VMEM((HEADS_V, ROWS, DK), F32),
            pltpu.VMEM((CHIPS, 2 * DK, DK), BF16),
            pltpu.VMEM((CHIPS, DK, DK), BF16),
            pltpu.VMEM((HEADS_V, DK, DK), BF16),
            pltpu.VMEM((HEADS_Q, ROWS, HEAD_WIDTH), BF16),
            pltpu.VMEM((SLOTS, ROWS, ROWS), F32),
            pltpu.VMEM((SLOTS, ROWS, ROWS), F32),
            pltpu.VMEM((ROWS, 128), F32),
            pltpu.VMEM((ROWS, 128), F32),
            pltpu.VMEM((SLOTS, ROWS, ROWS), F32),
            pltpu.VMEM((DK, DK), F32),
            pltpu.VMEM((HEADS_V, 2 * DK, DK), BF16),
            pltpu.VMEM((HEADS_V, 2 * DK, DK), BF16),
            dma, dma((2,)), dma, dma((SLOTS, 2)), dma, dma((GROUPS,)), dma, dma, dma, dma, dma, dma,
            pltpu.VMEM((ROWS, 2048), BF16),
            pltpu.VMEM((ROWS, 2048), BF16),
            pltpu.VMEM((ROWS, 1024), BF16),
            pltpu.VMEM((ROWS, 1024), BF16),
            pltpu.VMEM((ROWS, 2048), BF16),
            pltpu.VMEM((ROWS, 2048), BF16),
            dma((6,)),
        ],
        compiler_params=pltpu.CompilerParams(
            collective_id=0, has_side_effects=True, vmem_limit_bytes=56 * 2**20
        ),
    )(
        segment_ids.reshape(1, ROWS), freq,
        attn_query, attention_keys, attention_values, attn_gate, delta_query, delta_key,
        update_rule_payload, delta_beta.T, delta_decay.T, delta_gate, norm_gain.reshape(1, DK),
    )


def solution(mesh):
    rows = P(("dp", "ctx"))
    wide = P(("dp", "ctx"), None)
    return jax.shard_map(
        per_device,
        mesh=mesh,
        in_specs=(rows,) + (wide,) * 10 + (P(),),
        out_specs=(wide, wide),
        check_vma=False,
    )
```

```python
import jax
import jax.numpy as jnp
import numpy as np
from jax import lax
from jax.experimental import pallas as pl
from jax.experimental.pallas import tpu as pltpu
from jax.sharding import PartitionSpec as P

HEAD_WIDTH = 256
ROTARY_ENTRIES = 64
ROPE_THETA = 10000000.0
DK = 128
DOCS = 8
ROWS = 256
RANKS = 32
SLOTS = 17
HEADS_Q = 8
HEADS_K = 8
HEADS_V = 16
GROUPS = 4
PER = HEADS_K // GROUPS
MESH = pl.DeviceIdType.MESH
F32 = jnp.float32
BF16 = jnp.bfloat16
NEG = -1e30
LOG2E = 1.4426950408889634
CHIPS = 16
KEY, VALUE = 0, 1


def nn(a, b):
    return lax.dot_general(a, b, (((1,), (0,)), ((), ())), preferred_element_type=F32)


def nt(a, b):
    return lax.dot_general(a, b, (((1,), (1,)), ((), ())), preferred_element_type=F32)


def tn(a, b):
    return lax.dot_general(a, b, (((0,), (0,)), ((), ())), preferred_element_type=F32)


def iota(shape, dim):
    return lax.broadcasted_iota(jnp.int32, shape, dim)


def lanes(index, width):
    return pl.ds(pl.multiple_of(index * width, width), width)


def rotate(x, cos, sin):
    lane = iota(x.shape, 1)
    swapped = jnp.where(lane < 32, pltpu.roll(x, 96, 1), pltpu.roll(x, 32, 1))
    return x * cos + swapped * sin


def pair_diag(packed):
    zero = jnp.zeros((128, 128), packed.dtype)
    return jnp.concatenate(
        [
            jnp.concatenate([packed[:, :128], zero], axis=1),
            jnp.concatenate([zero, packed[:, 128:]], axis=1),
        ],
        axis=0,
    )


def inverses(lowers):
    row = iota((128, 256), 0)
    col = iota((128, 256), 1) % 128
    apart = row ^ col
    packed = [jnp.concatenate([x[:128, :128], x[128:, 128:]], axis=1) for x in lowers]
    inv = [jnp.where(apart == 0, 1.0, 0.0) - jnp.where(apart == 1, x, 0.0) for x in packed]
    block = 2
    while block < 128:
        here = (apart >= block) & (apart < 2 * block)
        off = [jnp.where(here, x, 0.0).astype(BF16) for x in packed]
        inv_b = [x.astype(BF16) for x in inv]
        left = [nn(x, pair_diag(c)) for x, c in zip(inv_b, off)]
        inv = [x - nn(c.astype(BF16), pair_diag(b)) for x, c, b in zip(inv, left, inv_b)]
        block *= 2
    inv_b = [x.astype(BF16) for x in inv]
    half = [nn(x[128:, :128].astype(BF16), b[:, :128]) for x, b in zip(lowers, inv_b)]
    corner = [nn(b[:, 128:], c.astype(BF16)) for b, c in zip(inv_b, half)]
    return [
        jnp.concatenate(
            [
                jnp.concatenate([b[:, :128], jnp.zeros((128, 128), BF16)], axis=1),
                jnp.concatenate([(-c).astype(BF16), b[:, 128:]], axis=1),
            ],
            axis=0,
        )
        for b, c in zip(inv_b, corner)
    ]


def kernel(
    seg_row, freq, q_hbm, k, v, gate_hbm, dq_hbm, dk_hbm, pv_hbm, beta, decay, dgate_hbm, gain,
    attn_out, delta_out,
    cnt, counts, kv, colg, colb, row_pack, mta, reach, intra, inbox, stage, state_in,
    qr, s_even, s_odd, top_even, top_odd, bias, state, twin, comb,
    cnt_send, cnt_recv, kv_send, kv_recv, twin_send, twin_recv, comb_send, comb_recv,
    st_send, st_recv, st2_send, st2_recv,
    q, gate, dq, dk, pv, dgate, in_sem,
):
    me = lax.axis_index("ctx")
    core = lax.rem(me, 2)
    chip = me // 2
    y = lax.rem(chip, 4)
    z = chip // 4

    def at(zz, yy, cc):
        return {"ctx": (lax.rem(zz, 4) * 4 + lax.rem(yy, 4)) * 2 + cc}

    barrier = pltpu.get_barrier_semaphore()

    @pl.loop(1, RANKS)
    def _(j):
        pl.semaphore_signal(
            barrier, inc=1, device_id={"ctx": lax.rem(me + j, RANKS)}, device_id_type=MESH
        )

    loads = [
        pltpu.make_async_copy(src, dst, in_sem.at[n])
        for n, (src, dst) in enumerate(
            [(q_hbm, q), (dq_hbm, dq), (dk_hbm, dk), (pv_hbm, pv), (gate_hbm, gate), (dgate_hbm, dgate)]
        )
    ]
    for load in loads:
        load.start()

    doc = iota((DOCS, ROWS), 0)
    mine = jnp.sum(jnp.where(seg_row[...] == doc, 1.0, 0.0), axis=1, keepdims=True)
    cnt[...] = jnp.broadcast_to(mine, (DOCS, 128))
    counts[0] = jnp.broadcast_to(mine, (DOCS, 128))
    lane1 = iota((ROWS, 128), 1)
    slot = (me * ROWS).astype(F32) + iota((ROWS, 1), 0).astype(F32)
    angle = slot * freq[...]
    cos = jnp.cos(angle)
    sin = jnp.sin(angle) * jnp.where(lane1 < 32, -1.0, 1.0)
    kv[0, KEY, :, :128] = rotate(k[:, :128].astype(F32), cos, sin).astype(BF16)
    kv[0, KEY, :, 128:] = k[:, 128:]
    kv[0, VALUE] = v[...]
    pl.semaphore_wait(barrier, RANKS - 1)

    def send_kv(part, src, dst, target):
        pltpu.make_async_remote_copy(
            kv.at[src, part], kv.at[dst, part], kv_send, kv_recv.at[dst, part],
            device_id=target, device_id_type=MESH,
        ).start()

    def got_kv(part, j):
        pltpu.make_async_copy(kv.at[j, part], kv.at[j, part], kv_recv.at[j, part]).wait()

    def to_twin(part, d):
        send_kv(part, 2 * d, 2 * d + 1 - 2 * core, at(z, y, 1 - core))

    def send_above(part):
        send_kv(part, 0, 8, at(z + 1, y, core))

    def send_own(part):
        for m in (1, 3, 2):

            @pl.when(y + m < 4)
            def _():
                send_kv(part, 0, 2 * m, at(z, y + m, core))

        @pl.when(core == 0)
        def _():
            to_twin(part, 0)

    def slot_of(source, m):
        return 2 * (4 + m - 4 * ((source + m) // 4))

    hop = (3, 1)
    behind = [lax.rem(y + 4 - t, 4) for t in hop]
    passed = [slot_of(b, t) for b, t in zip(behind, hop)]

    def relay_above(part):
        got_kv(part, 8)
        for m in (1, 3):
            send_kv(part, 8, slot_of(y, m), at(z, y + m, core))
        to_twin(part, 4)

    def relay_second(part):
        got_kv(part, 16)
        for m in (3, 1, 2):

            @pl.when(y + m >= 4)
            def _():
                send_kv(part, 16, 2 * (m + 4), at(z, y + m, core))

        @pl.when(core == 1)
        def _():
            to_twin(part, 8)

    def relay_passed(part):
        got_kv(part, passed[part])
        send_kv(part, passed[part], slot_of(behind[part], 2), at(z, y + hop[part], core))
        to_twin(part, passed[part] // 2)

    def relay_rest(part):
        for d in (1, 2, 3, 5, 6, 7):

            @pl.when(passed[part] != 2 * d)
            def _():
                got_kv(part, 2 * d)
                to_twin(part, d)

    def relay_last():
        for d in range(8):
            got_kv(KEY, 2 * d + 1)
            got_kv(VALUE, 2 * d + 1)

    @pl.loop(1, RANKS)
    def _(j):
        pltpu.make_async_remote_copy(
            cnt, counts.at[j], cnt_send, cnt_recv.at[jnp.minimum(j - 1, 1)],
            device_id={"ctx": lax.rem(me + j, RANKS)}, device_id_type=MESH,
        ).start()

    send_above(VALUE)
    send_above(KEY)
    send_own(VALUE)
    send_own(KEY)
    sums_of = jnp.where(iota((ROWS, ROWS), 0) <= iota((ROWS, ROWS), 1), 1.0, 0.0).astype(BF16)
    dec = decay[...]
    hi = dec.astype(BF16)
    mid = (dec - hi.astype(F32)).astype(BF16)
    low = (dec - hi.astype(F32) - mid.astype(F32)).astype(BF16)
    sums = nn(hi, sums_of) + nn(mid, sums_of) + nn(low, sums_of)
    row_pack[...] = sums
    seg_f = seg_row[...].astype(F32)
    pack = jnp.concatenate(
        [
            sums, beta[...],
            jnp.broadcast_to(seg_f, (96, ROWS)),
        ],
        axis=0,
    )
    columns = pack.T
    seg = columns[:, 32:33].astype(jnp.int32)
    for g in range(GROUPS):
        w = 2 * PER
        colg[g, :, :w] = columns[:, g * w : (g + 1) * w]
        colb[g, :, :w] = columns[:, 16 + g * w : 16 + (g + 1) * w]

    relay_above(VALUE)
    send_kv(VALUE, 0, 16, at(z + 2, y, core))
    send_kv(KEY, 0, 16, at(z + 2, y, core))

    loads[0].wait()
    for h in range(HEADS_Q):
        base = h * HEAD_WIDTH
        qr[h, :, :128] = rotate(q[:, base : base + 128].astype(F32), cos, sin).astype(BF16)
        qr[h, :, 128:] = q[:, base + 128 : base + 256]

    pltpu.make_async_copy(counts.at[1], counts.at[1], cnt_recv.at[0]).wait()
    held = jnp.where(counts[1] > 0.0, iota((DOCS, 128), 0).astype(F32), -1.0)
    held = jnp.where(me > 0, jnp.max(held, axis=0, keepdims=True), -1.0)
    first_doc = jnp.where(seg.astype(F32) == held[:, :1], 1.0, 0.0)
    row2 = iota((ROWS, ROWS), 0)
    col2 = iota((ROWS, ROWS), 1)
    same = (seg == seg_row[...]) & (row2 >= col2)
    seg_last = seg[ROWS - 1 : ROWS, :]
    last_doc = jnp.where(seg == seg_last, 1.0, 0.0)
    eye = jnp.where(iota((DK, DK), 0) == iota((DK, DK), 1), 1.0, 0.0)

    relay_above(KEY)

    def group(g):
        parts = []
        for i in range(PER):
            kh = g * PER + i
            kr = dk[:, lanes(kh, DK)]
            qx = dq[:, lanes(kh, DK)]
            kf = kr.astype(F32)
            qf = qx.astype(F32)
            rk = lax.rsqrt(jnp.sum(kf * kf, axis=1, keepdims=True) + 1e-06)
            rq = lax.rsqrt(jnp.sum(qf * qf, axis=1, keepdims=True) + 1e-06) * DK ** (-0.5)
            rk_row = jnp.broadcast_to(rk, (ROWS, 128)).T[0:1]
            gram = nt(kr, kr) * (rk * rk_row)
            probe = nt(qx, kr) * (rq * rk_row)
            for n in range(2):
                gc = colg[g][:, 2 * i + n : 2 * i + n + 1]
                bc = colb[g][:, 2 * i + n : 2 * i + n + 1]
                gr = row_pack[pl.ds(2 * kh + n, 1), :]
                span = jnp.where(same, jnp.exp(jnp.minimum(gc - gr, 0.0)), 0.0)
                parts.append((2 * kh + n, kf * rk, qf * rq, gc, bc, (span * gram) * bc, (span * probe).astype(BF16)))
        solved = inverses([p[5] for p in parts])

        @pl.when(g == 0)
        def _():
            relay_passed(VALUE)

        @pl.when(g == 1)
        def _():
            relay_passed(KEY)

        wus = []
        for (h, kn, qn, gc, bc, _, _), inv in zip(parts, solved):
            entry = first_doc * jnp.exp(gc)
            vf = pv[:, lanes(h, DK)].astype(F32)
            right = jnp.concatenate([kn * (bc * entry), vf * bc], axis=1).astype(BF16)
            wus.append(nn(inv, right).astype(BF16))
        inners = [nn(p[6], wu) for p, wu in zip(parts, wus)]
        boths = []
        for (h, kn, qn, gc, bc, _, _), wu in zip(parts, wus):
            tail = last_doc * jnp.exp(jnp.minimum(gc[ROWS - 1 : ROWS] - gc, 0.0))
            boths.append(tn(wu, (kn * tail).astype(BF16)))
        for (h, kn, qn, gc, bc, _, _), inner, both in zip(parts, inners, boths):
            entry = first_doc * jnp.exp(gc)
            reach[h] = (qn * entry - inner[:, :DK]).astype(BF16)
            intra[h] = inner[:, DK:]
            mt = eye * entry[ROWS - 1 : ROWS] - both[:DK]
            mta[h] = jnp.concatenate([mt, both[DK:]], axis=0).astype(BF16)

    heads = 2 * PER

    def send_heads(g):
        @pl.when(core == 0)
        def _():
            pltpu.make_async_remote_copy(
                mta.at[pl.ds(g * heads, heads)], twin.at[pl.ds(g * heads, heads)],
                twin_send, twin_recv.at[g],
                device_id={"ctx": me + 1}, device_id_type=MESH,
            ).start()

        @pl.when(core == 1)
        def _():
            pltpu.make_async_copy(
                twin.at[pl.ds(g * heads, heads)], twin.at[pl.ds(g * heads, heads)], twin_recv.at[g]
            ).wait()

            hs = [g * heads + i for i in range(heads)]
            pairs = [nn(twin[h], mta[h, :DK]) for h in hs]
            for h, both in zip(hs, pairs):
                comb[h, :DK] = both[:DK].astype(BF16)
                comb[h, DK:] = (both[DK:] + mta[h, DK:].astype(F32)).astype(BF16)
            for h in hs:
                pltpu.make_async_remote_copy(
                    comb.at[h], inbox.at[lax.rem(chip - h + CHIPS, CHIPS)], comb_send, comb_recv,
                    device_id={"ctx": 2 * h}, device_id_type=MESH,
                ).start()

    for load in loads[1:4]:
        load.wait()

    @pl.loop(0, GROUPS)
    def _(g):
        group(g)

        @pl.when(g == 0)
        def _():
            relay_second(VALUE)

        @pl.when(g == 1)
        def _():
            relay_second(KEY)

        @pl.when(g == 2)
        def _():
            relay_rest(VALUE)

        @pl.when(g == 3)
        def _():
            relay_rest(KEY)

        send_heads(g)

    relay_last()

    pltpu.make_async_copy(
        counts.at[pl.ds(2, RANKS - 2)], counts.at[pl.ds(2, RANKS - 2)], cnt_recv.at[1]
    ).wait()
    totals = jnp.sum(counts[...], axis=0)
    totals = jnp.concatenate([totals, totals], axis=1)
    start_row = jnp.sum(jnp.where(doc < seg_row[...], totals, 0.0), axis=0, keepdims=True)
    starts = jnp.broadcast_to(start_row, (128, ROWS)).T[:, :1]
    pos0 = iota((ROWS, ROWS), 1).astype(F32)
    for j in range(SLOTS):
        allowed = (pos0 + ((me - j) * ROWS).astype(F32)) >= starts
        if j == 0:
            allowed = allowed & (row2 >= col2)
        bias[j] = jnp.where(allowed, 0.0, NEG)

    def overlap(low, now, now_top, later, later_top):
        nxt = jnp.minimum(low + 1, HEADS_Q - 1)
        best = total = acc = None
        if now is not None:
            top = now_top[...]
            top = jnp.concatenate([top, top], axis=1)
        for j in range(SLOTS):
            if later is not None:
                s = nt(qr[nxt], kv[j, 0]) + bias[j]
                later[j] = s
                m2 = jnp.maximum(s[:, :128], s[:, 128:])
                best = m2 if best is None else jnp.maximum(best, m2)
            if now is not None:
                w = jnp.exp2((now[j] - top) * (LOG2E * HEAD_WIDTH ** (-0.5)))
                t2 = w[:, :128] + w[:, 128:]
                total = t2 if total is None else total + t2
                part = nn(w.astype(BF16), kv[j, 1])
                acc = part if acc is None else acc + part
        if later is not None:
            later_top[...] = jnp.broadcast_to(jnp.max(best, axis=1, keepdims=True), (ROWS, 128))
        if now is not None:
            total = jnp.sum(total, axis=1, keepdims=True)
            gt = gate[:, lanes(low, HEAD_WIDTH)].astype(F32)
            attn_out[:, lanes(low, HEAD_WIDTH)] = (
                acc * (1.0 / total) * jax.nn.sigmoid(gt)
            ).astype(BF16)

    def two_heads(i):
        overlap(2 * i, s_even, top_even, s_odd, top_odd)
        overlap(2 * i + 1, s_odd, top_odd, s_even, top_even)

    overlap(-1, None, None, s_even, top_even)
    loads[4].wait()
    loads[5].wait()

    @pl.loop(0, 4)
    def _(i):
        two_heads(i)

        @pl.when((core == 0) & (i == 1))
        def _():
            pltpu.make_async_copy(inbox, inbox, comb_recv).wait()
            state[...] = jnp.zeros((DK, DK), F32)

            @pl.loop(0, CHIPS)
            def _(c):
                j = lax.rem(c - chip + CHIPS, CHIPS)
                stage[j] = state[...].astype(BF16)
                state[...] = nn(stage[j], inbox[j, :DK]) + inbox[j, DK:].astype(F32)

                @pl.when(j != 0)
                def _():
                    pltpu.make_async_remote_copy(
                        stage.at[j], state_in.at[chip], st_send, st_recv,
                        device_id={"ctx": 2 * c}, device_id_type=MESH,
                    ).start()

                @pl.when(j == 0)
                def _():
                    state_in[chip] = stage[0]

        @pl.when((core == 0) & (i == 2))
        def _():
            pltpu.make_async_copy(state_in.at[pl.ds(0, 15)], state_in.at[pl.ds(0, 15)], st_recv).wait()
            pltpu.make_async_remote_copy(
                state_in, state_in, st2_send, st2_recv,
                device_id={"ctx": me + 1}, device_id_type=MESH,
            ).start()

    @pl.when(core == 1)
    def _():
        pltpu.make_async_copy(state_in, state_in, st2_recv).wait()

        @pl.loop(0, HEADS_V // 8)
        def _(t):
            hs = [8 * t + i for i in range(8)]
            moved = [nn(state_in[h], twin[h, :DK]) + twin[h, DK:].astype(F32) for h in hs]
            for h, later in zip(hs, moved):
                state_in[h] = later.astype(BF16)

        pltpu.make_async_copy(comb, comb, comb_send).wait()

    @pl.loop(0, HEADS_V // 4)
    def _(t):
        for i in range(4):
            h = 4 * t + i
            out = intra[h] + nt(reach[h], state_in[h])
            spread = lax.rsqrt(jnp.mean(out * out, axis=1, keepdims=True) + 1e-06)
            gt = dgate[:, lanes(h, DK)].astype(F32)
            res = out * spread * gain[...] * (gt * jax.nn.sigmoid(gt))
            delta_out[:, lanes(h, DK)] = res.astype(BF16)

    @pl.when(core == 0)
    def _():
        pltpu.make_async_copy(mta, mta, twin_send).wait()
        pltpu.make_async_copy(stage.at[pl.ds(1, 15)], stage.at[pl.ds(1, 15)], st_send).wait()
        pltpu.make_async_copy(state_in, state_in, st2_send).wait()

    pltpu.make_async_copy(counts.at[pl.ds(1, 31)], counts.at[pl.ds(1, 31)], cnt_send).wait()

    pltpu.make_async_copy(kv.at[pl.ds(1, 16)], kv.at[pl.ds(1, 16)], kv_send).wait()


def per_device(
    segment_ids, attn_query, attention_keys, attention_values, attn_gate, delta_query, delta_key,
    update_rule_payload, delta_beta, delta_decay, delta_gate, norm_gain,
):
    entry = np.arange(128)
    freq = np.where(
        entry < ROTARY_ENTRIES, ROPE_THETA ** (-2.0 * (entry % 32) / ROTARY_ENTRIES), 0.0
    ).astype(np.float32)[None]
    vmem = pl.BlockSpec(memory_space=pltpu.VMEM)
    hbm = pl.BlockSpec(memory_space=pl.ANY)
    dma = pltpu.SemaphoreType.DMA
    wide = jax.ShapeDtypeStruct((ROWS, 2048), BF16)
    return pl.pallas_call(
        kernel,
        out_shape=(wide, wide),
        in_specs=[vmem, vmem, hbm, vmem, vmem, hbm, hbm, hbm, hbm, vmem, vmem, hbm, vmem],
        out_specs=(vmem, vmem),
        scratch_shapes=[
            pltpu.VMEM((8, 128), F32),
            pltpu.VMEM((RANKS, 8, 128), F32),
            pltpu.VMEM((SLOTS, 2, ROWS, HEAD_WIDTH), BF16),
            pltpu.VMEM((GROUPS, ROWS, 2 * PER), F32),
            pltpu.VMEM((GROUPS, ROWS, 2 * PER), F32),
            pltpu.VMEM((HEADS_V, ROWS), F32),
            pltpu.VMEM((HEADS_V, 2 * DK, DK), BF16),
            pltpu.VMEM((HEADS_V, ROWS, DK), BF16),
            pltpu.VMEM((HEADS_V, ROWS, DK), F32),
            pltpu.VMEM((CHIPS, 2 * DK, DK), BF16),
            pltpu.VMEM((CHIPS, DK, DK), BF16),
            pltpu.VMEM((HEADS_V, DK, DK), BF16),
            pltpu.VMEM((HEADS_Q, ROWS, HEAD_WIDTH), BF16),
            pltpu.VMEM((SLOTS, ROWS, ROWS), F32),
            pltpu.VMEM((SLOTS, ROWS, ROWS), F32),
            pltpu.VMEM((ROWS, 128), F32),
            pltpu.VMEM((ROWS, 128), F32),
            pltpu.VMEM((SLOTS, ROWS, ROWS), F32),
            pltpu.VMEM((DK, DK), F32),
            pltpu.VMEM((HEADS_V, 2 * DK, DK), BF16),
            pltpu.VMEM((HEADS_V, 2 * DK, DK), BF16),
            dma, dma((2,)), dma, dma((SLOTS, 2)), dma, dma((GROUPS,)), dma, dma, dma, dma, dma, dma,
            pltpu.VMEM((ROWS, 2048), BF16),
            pltpu.VMEM((ROWS, 2048), BF16),
            pltpu.VMEM((ROWS, 1024), BF16),
            pltpu.VMEM((ROWS, 1024), BF16),
            pltpu.VMEM((ROWS, 2048), BF16),
            pltpu.VMEM((ROWS, 2048), BF16),
            dma((6,)),
        ],
        compiler_params=pltpu.CompilerParams(
            collective_id=0, has_side_effects=True, vmem_limit_bytes=56 * 2**20
        ),
    )(
        segment_ids.reshape(1, ROWS), freq,
        attn_query, attention_keys, attention_values, attn_gate, delta_query, delta_key,
        update_rule_payload, delta_beta.T, delta_decay.T, delta_gate, norm_gain.reshape(1, DK),
    )


def solution(mesh):
    rows = P(("dp", "ctx"))
    wide = P(("dp", "ctx"), None)
    return jax.shard_map(
        per_device,
        mesh=mesh,
        in_specs=(rows,) + (wide,) * 10 + (P(),),
        out_specs=(wide, wide),
        check_vma=False,
    )
```

```python
import jax
import jax.numpy as jnp
import numpy as np
from jax import lax
from jax.experimental import pallas as pl
from jax.experimental.pallas import tpu as pltpu
from jax.sharding import PartitionSpec as P

HEAD_WIDTH = 256
ROTARY_ENTRIES = 64
ROPE_THETA = 10000000.0
DK = 128
DOCS = 8
ROWS = 256
RANKS = 32
SLOTS = 17
HEADS_Q = 8
HEADS_K = 8
HEADS_V = 16
GROUPS = 4
PER = HEADS_K // GROUPS
MESH = pl.DeviceIdType.MESH
F32 = jnp.float32
BF16 = jnp.bfloat16
NEG = -1e30
LOG2E = 1.4426950408889634
CHIPS = 16
KEY, VALUE = 0, 1


def nn(a, b):
    return lax.dot_general(a, b, (((1,), (0,)), ((), ())), preferred_element_type=F32)


def nt(a, b):
    return lax.dot_general(a, b, (((1,), (1,)), ((), ())), preferred_element_type=F32)


def tn(a, b):
    return lax.dot_general(a, b, (((0,), (0,)), ((), ())), preferred_element_type=F32)


def iota(shape, dim):
    return lax.broadcasted_iota(jnp.int32, shape, dim)


def lanes(index, width):
    return pl.ds(pl.multiple_of(index * width, width), width)


def rotate(x, cos, sin):
    lane = iota(x.shape, 1)
    swapped = jnp.where(lane < 32, pltpu.roll(x, 96, 1), pltpu.roll(x, 32, 1))
    return x * cos + swapped * sin


def pair_diag(packed):
    zero = jnp.zeros((128, 128), packed.dtype)
    return jnp.concatenate(
        [
            jnp.concatenate([packed[:, :128], zero], axis=1),
            jnp.concatenate([zero, packed[:, 128:]], axis=1),
        ],
        axis=0,
    )


def inverses(lowers):
    row = iota((128, 256), 0)
    col = iota((128, 256), 1) % 128
    apart = row ^ col
    packed = [jnp.concatenate([x[:128, :128], x[128:, 128:]], axis=1) for x in lowers]
    inv = [jnp.where(apart == 0, 1.0, 0.0) - jnp.where(apart == 1, x, 0.0) for x in packed]
    block = 2
    while block < 128:
        here = (apart >= block) & (apart < 2 * block)
        off = [jnp.where(here, x, 0.0).astype(BF16) for x in packed]
        inv_b = [x.astype(BF16) for x in inv]
        left = [nn(x, pair_diag(c)) for x, c in zip(inv_b, off)]
        inv = [x - nn(c.astype(BF16), pair_diag(b)) for x, c, b in zip(inv, left, inv_b)]
        block *= 2
    inv_b = [x.astype(BF16) for x in inv]
    half = [nn(x[128:, :128].astype(BF16), b[:, :128]) for x, b in zip(lowers, inv_b)]
    corner = [nn(b[:, 128:], c.astype(BF16)) for b, c in zip(inv_b, half)]
    return [
        jnp.concatenate(
            [
                jnp.concatenate([b[:, :128], jnp.zeros((128, 128), BF16)], axis=1),
                jnp.concatenate([(-c).astype(BF16), b[:, 128:]], axis=1),
            ],
            axis=0,
        )
        for b, c in zip(inv_b, corner)
    ]


def kernel(
    seg_row, freq, q_hbm, k, v, gate_hbm, dq_hbm, dk_hbm, pv_hbm, beta, decay, dgate_hbm, gain,
    attn_out, delta_out,
    cnt, counts, kv, colg, colb, row_pack, mta, reach, intra, inbox, stage, state_in,
    qr, s_even, s_odd, top_even, top_odd, bias, state, twin, comb,
    cnt_send, cnt_recv, kv_send, kv_recv, twin_send, twin_recv, comb_send, comb_recv,
    st_send, st_recv, st2_send, st2_recv,
    q, gate, dq, dk, pv, dgate, in_sem,
):
    me = lax.axis_index("ctx")
    core = lax.rem(me, 2)
    chip = me // 2
    y = lax.rem(chip, 4)
    z = chip // 4

    def at(zz, yy, cc):
        return {"ctx": (lax.rem(zz, 4) * 4 + lax.rem(yy, 4)) * 2 + cc}

    barrier = pltpu.get_barrier_semaphore()

    @pl.loop(1, RANKS)
    def _(j):
        pl.semaphore_signal(
            barrier, inc=1, device_id={"ctx": lax.rem(me + j, RANKS)}, device_id_type=MESH
        )

    loads = [
        pltpu.make_async_copy(src, dst, in_sem.at[n])
        for n, (src, dst) in enumerate(
            [(q_hbm, q), (dq_hbm, dq), (dk_hbm, dk), (pv_hbm, pv), (gate_hbm, gate), (dgate_hbm, dgate)]
        )
    ]
    for load in loads:
        load.start()

    doc = iota((DOCS, ROWS), 0)
    mine = jnp.sum(jnp.where(seg_row[...] == doc, 1.0, 0.0), axis=1, keepdims=True)
    cnt[...] = jnp.broadcast_to(mine, (DOCS, 128))
    counts[0] = jnp.broadcast_to(mine, (DOCS, 128))
    lane1 = iota((ROWS, 128), 1)
    slot = (me * ROWS).astype(F32) + iota((ROWS, 1), 0).astype(F32)
    angle = slot * freq[...]
    cos = jnp.cos(angle)
    sin = jnp.sin(angle) * jnp.where(lane1 < 32, -1.0, 1.0)
    kv[0, KEY, :, :128] = rotate(k[:, :128].astype(F32), cos, sin).astype(BF16)
    kv[0, KEY, :, 128:] = k[:, 128:]
    kv[0, VALUE] = v[...]
    pl.semaphore_wait(barrier, RANKS - 1)

    def send_kv(part, src, dst, target):
        pltpu.make_async_remote_copy(
            kv.at[src, part], kv.at[dst, part], kv_send, kv_recv.at[dst, part],
            device_id=target, device_id_type=MESH,
        ).start()

    def got_kv(part, j):
        pltpu.make_async_copy(kv.at[j, part], kv.at[j, part], kv_recv.at[j, part]).wait()

    def to_twin(part, d):
        send_kv(part, 2 * d, 2 * d + 1 - 2 * core, at(z, y, 1 - core))

    def send_above(part):
        send_kv(part, 0, 8, at(z + 1, y, core))

    def send_own(part):
        for m in (1, 3, 2):

            @pl.when(y + m < 4)
            def _():
                send_kv(part, 0, 2 * m, at(z, y + m, core))

        @pl.when(core == 0)
        def _():
            to_twin(part, 0)

    def slot_of(source, m):
        return 2 * (4 + m - 4 * ((source + m) // 4))

    hop = (3, 1)
    behind = [lax.rem(y + 4 - t, 4) for t in hop]
    passed = [slot_of(b, t) for b, t in zip(behind, hop)]

    def relay_above(part):
        got_kv(part, 8)
        for m in (1, 3):
            send_kv(part, 8, slot_of(y, m), at(z, y + m, core))
        to_twin(part, 4)

    def relay_second(part):
        got_kv(part, 16)
        for m in (3, 1, 2):

            @pl.when(y + m >= 4)
            def _():
                send_kv(part, 16, 2 * (m + 4), at(z, y + m, core))

        @pl.when(core == 1)
        def _():
            to_twin(part, 8)

    def relay_passed(part):
        got_kv(part, passed[part])
        send_kv(part, passed[part], slot_of(behind[part], 2), at(z, y + hop[part], core))
        to_twin(part, passed[part] // 2)

    def relay_rest(part):
        for d in (1, 2, 3, 5, 6, 7):

            @pl.when(passed[part] != 2 * d)
            def _():
                got_kv(part, 2 * d)
                to_twin(part, d)

    def relay_last():
        for d in range(8):
            got_kv(KEY, 2 * d + 1)
            got_kv(VALUE, 2 * d + 1)

    @pl.loop(1, RANKS)
    def _(j):
        pltpu.make_async_remote_copy(
            cnt, counts.at[j], cnt_send, cnt_recv.at[jnp.minimum(j - 1, 1)],
            device_id={"ctx": lax.rem(me + j, RANKS)}, device_id_type=MESH,
        ).start()

    send_above(VALUE)
    send_above(KEY)
    send_own(VALUE)
    send_own(KEY)
    sums_of = jnp.where(iota((ROWS, ROWS), 0) <= iota((ROWS, ROWS), 1), 1.0, 0.0).astype(BF16)
    dec = decay[...]
    hi = dec.astype(BF16)
    mid = (dec - hi.astype(F32)).astype(BF16)
    low = (dec - hi.astype(F32) - mid.astype(F32)).astype(BF16)
    sums = nn(hi, sums_of) + nn(mid, sums_of) + nn(low, sums_of)
    row_pack[...] = sums
    seg_f = seg_row[...].astype(F32)
    pack = jnp.concatenate(
        [
            sums, beta[...],
            jnp.broadcast_to(seg_f, (96, ROWS)),
        ],
        axis=0,
    )
    columns = pack.T
    seg = columns[:, 32:33].astype(jnp.int32)
    for g in range(GROUPS):
        w = 2 * PER
        colg[g, :, :w] = columns[:, g * w : (g + 1) * w]
        colb[g, :, :w] = columns[:, 16 + g * w : 16 + (g + 1) * w]

    relay_above(VALUE)
    send_kv(VALUE, 0, 16, at(z + 2, y, core))
    send_kv(KEY, 0, 16, at(z + 2, y, core))

    loads[0].wait()
    for h in range(HEADS_Q):
        base = h * HEAD_WIDTH
        qr[h, :, :128] = rotate(q[:, base : base + 128].astype(F32), cos, sin).astype(BF16)
        qr[h, :, 128:] = q[:, base + 128 : base + 256]

    pltpu.make_async_copy(counts.at[1], counts.at[1], cnt_recv.at[0]).wait()
    held = jnp.where(counts[1] > 0.0, iota((DOCS, 128), 0).astype(F32), -1.0)
    held = jnp.where(me > 0, jnp.max(held, axis=0, keepdims=True), -1.0)
    first_doc = jnp.where(seg.astype(F32) == held[:, :1], 1.0, 0.0)
    row2 = iota((ROWS, ROWS), 0)
    col2 = iota((ROWS, ROWS), 1)
    same = (seg == seg_row[...]) & (row2 >= col2)
    seg_last = seg[ROWS - 1 : ROWS, :]
    last_doc = jnp.where(seg == seg_last, 1.0, 0.0)
    eye = jnp.where(iota((DK, DK), 0) == iota((DK, DK), 1), 1.0, 0.0)

    relay_above(KEY)

    def group(g):
        parts = []
        for i in range(PER):
            kh = g * PER + i
            kr = dk[:, lanes(kh, DK)]
            qx = dq[:, lanes(kh, DK)]
            kf = kr.astype(F32)
            qf = qx.astype(F32)
            rk = lax.rsqrt(jnp.sum(kf * kf, axis=1, keepdims=True) + 1e-06)
            rq = lax.rsqrt(jnp.sum(qf * qf, axis=1, keepdims=True) + 1e-06) * DK ** (-0.5)
            rk_row = jnp.broadcast_to(rk, (ROWS, 128)).T[0:1]
            gram = nt(kr, kr) * (rk * rk_row)
            probe = nt(qx, kr) * (rq * rk_row)
            for n in range(2):
                gc = colg[g][:, 2 * i + n : 2 * i + n + 1]
                bc = colb[g][:, 2 * i + n : 2 * i + n + 1]
                gr = row_pack[pl.ds(2 * kh + n, 1), :]
                span = jnp.where(same, jnp.exp(jnp.minimum(gc - gr, 0.0)), 0.0)
                parts.append((2 * kh + n, kf * rk, qf * rq, gc, bc, (span * gram) * bc, (span * probe).astype(BF16)))
        solved = inverses([p[5] for p in parts])

        @pl.when(g == 0)
        def _():
            relay_passed(VALUE)

        @pl.when(g == 1)
        def _():
            relay_passed(KEY)

        wus = []
        for (h, kn, qn, gc, bc, _, _), inv in zip(parts, solved):
            entry = first_doc * jnp.exp(gc)
            vf = pv[:, lanes(h, DK)].astype(F32)
            right = jnp.concatenate([kn * (bc * entry), vf * bc], axis=1).astype(BF16)
            wus.append(nn(inv, right).astype(BF16))
        inners = [nn(p[6], wu) for p, wu in zip(parts, wus)]
        boths = []
        for (h, kn, qn, gc, bc, _, _), wu in zip(parts, wus):
            tail = last_doc * jnp.exp(jnp.minimum(gc[ROWS - 1 : ROWS] - gc, 0.0))
            boths.append(tn(wu, (kn * tail).astype(BF16)))
        for (h, kn, qn, gc, bc, _, _), inner, both in zip(parts, inners, boths):
            entry = first_doc * jnp.exp(gc)
            reach[h] = (qn * entry - inner[:, :DK]).astype(BF16)
            intra[h] = inner[:, DK:]
            mt = eye * entry[ROWS - 1 : ROWS] - both[:DK]
            mta[h] = jnp.concatenate([mt, both[DK:]], axis=0).astype(BF16)

    heads = 2 * PER

    def send_heads(g):
        @pl.when(core == 0)
        def _():
            pltpu.make_async_remote_copy(
                mta.at[pl.ds(g * heads, heads)], twin.at[pl.ds(g * heads, heads)],
                twin_send, twin_recv.at[g],
                device_id={"ctx": me + 1}, device_id_type=MESH,
            ).start()

        @pl.when(core == 1)
        def _():
            pltpu.make_async_copy(
                twin.at[pl.ds(g * heads, heads)], twin.at[pl.ds(g * heads, heads)], twin_recv.at[g]
            ).wait()

            hs = [g * heads + i for i in range(heads)]
            pairs = [nn(twin[h], mta[h, :DK]) for h in hs]
            for h, both in zip(hs, pairs):
                comb[h, :DK] = both[:DK].astype(BF16)
                comb[h, DK:] = (both[DK:] + mta[h, DK:].astype(F32)).astype(BF16)
            for h in hs:
                pltpu.make_async_remote_copy(
                    comb.at[h], inbox.at[lax.rem(chip - h + CHIPS, CHIPS)], comb_send, comb_recv,
                    device_id={"ctx": 2 * h}, device_id_type=MESH,
                ).start()

    for load in loads[1:4]:
        load.wait()

    @pl.loop(0, GROUPS)
    def _(g):
        group(g)

        @pl.when(g == 0)
        def _():
            relay_second(VALUE)

        @pl.when(g == 1)
        def _():
            relay_second(KEY)

        @pl.when(g == 2)
        def _():
            relay_rest(VALUE)

        @pl.when(g == 3)
        def _():
            relay_rest(KEY)

        send_heads(g)

    relay_last()

    pltpu.make_async_copy(
        counts.at[pl.ds(2, RANKS - 2)], counts.at[pl.ds(2, RANKS - 2)], cnt_recv.at[1]
    ).wait()
    totals = jnp.sum(counts[...], axis=0)
    totals = jnp.concatenate([totals, totals], axis=1)
    start_row = jnp.sum(jnp.where(doc < seg_row[...], totals, 0.0), axis=0, keepdims=True)
    starts = jnp.broadcast_to(start_row, (128, ROWS)).T[:, :1]
    pos0 = iota((ROWS, ROWS), 1).astype(F32)
    for j in range(SLOTS):
        allowed = (pos0 + ((me - j) * ROWS).astype(F32)) >= starts
        if j == 0:
            allowed = allowed & (row2 >= col2)
        bias[j] = jnp.where(allowed, 0.0, NEG)

    def overlap(low, now, now_top, later, later_top):
        nxt = jnp.minimum(low + 1, HEADS_Q - 1)
        best = total = acc = None
        if now is not None:
            top = now_top[...]
            top = jnp.concatenate([top, top], axis=1)
        for j in range(SLOTS):
            if later is not None:
                s = nt(qr[nxt], kv[j, 0]) + bias[j]
                later[j] = s
                m2 = jnp.maximum(s[:, :128], s[:, 128:])
                best = m2 if best is None else jnp.maximum(best, m2)
            if now is not None:
                w = jnp.exp2((now[j] - top) * (LOG2E * HEAD_WIDTH ** (-0.5)))
                t2 = w[:, :128] + w[:, 128:]
                total = t2 if total is None else total + t2
                part = nn(w.astype(BF16), kv[j, 1])
                acc = part if acc is None else acc + part
        if later is not None:
            later_top[...] = jnp.broadcast_to(jnp.max(best, axis=1, keepdims=True), (ROWS, 128))
        if now is not None:
            total = jnp.sum(total, axis=1, keepdims=True)
            gt = gate[:, lanes(low, HEAD_WIDTH)].astype(F32)
            attn_out[:, lanes(low, HEAD_WIDTH)] = (
                acc * (1.0 / total) * jax.nn.sigmoid(gt)
            ).astype(BF16)

    def two_heads(i):
        overlap(2 * i, s_even, top_even, s_odd, top_odd)
        overlap(2 * i + 1, s_odd, top_odd, s_even, top_even)

    overlap(-1, None, None, s_even, top_even)
    loads[4].wait()
    loads[5].wait()

    @pl.loop(0, 4)
    def _(i):
        two_heads(i)

        @pl.when((core == 0) & (i == 1))
        def _():
            pltpu.make_async_copy(inbox, inbox, comb_recv).wait()
            state[...] = jnp.zeros((DK, DK), F32)

            @pl.loop(0, CHIPS)
            def _(c):
                j = lax.rem(c - chip + CHIPS, CHIPS)
                stage[j] = state[...].astype(BF16)
                state[...] = nn(stage[j], inbox[j, :DK]) + inbox[j, DK:].astype(F32)

                @pl.when(j != 0)
                def _():
                    pltpu.make_async_remote_copy(
                        stage.at[j], state_in.at[chip], st_send, st_recv,
                        device_id={"ctx": 2 * c}, device_id_type=MESH,
                    ).start()

                @pl.when(j == 0)
                def _():
                    state_in[chip] = stage[0]

        @pl.when((core == 0) & (i == 2))
        def _():
            pltpu.make_async_copy(state_in.at[pl.ds(0, 15)], state_in.at[pl.ds(0, 15)], st_recv).wait()
            pltpu.make_async_remote_copy(
                state_in, state_in, st2_send, st2_recv,
                device_id={"ctx": me + 1}, device_id_type=MESH,
            ).start()

    @pl.when(core == 1)
    def _():
        pltpu.make_async_copy(state_in, state_in, st2_recv).wait()

        @pl.loop(0, HEADS_V // 8)
        def _(t):
            hs = [8 * t + i for i in range(8)]
            moved = [nn(state_in[h], twin[h, :DK]) + twin[h, DK:].astype(F32) for h in hs]
            for h, later in zip(hs, moved):
                state_in[h] = later.astype(BF16)

        pltpu.make_async_copy(comb, comb, comb_send).wait()

    @pl.loop(0, HEADS_V // 4)
    def _(t):
        for i in range(4):
            h = 4 * t + i
            out = intra[h] + nt(reach[h], state_in[h])
            spread = lax.rsqrt(jnp.mean(out * out, axis=1, keepdims=True) + 1e-06)
            gt = dgate[:, lanes(h, DK)].astype(F32)
            res = out * spread * gain[...] * (gt * jax.nn.sigmoid(gt))
            delta_out[:, lanes(h, DK)] = res.astype(BF16)

    @pl.when(core == 0)
    def _():
        pltpu.make_async_copy(mta, mta, twin_send).wait()
        pltpu.make_async_copy(stage.at[pl.ds(1, 15)], stage.at[pl.ds(1, 15)], st_send).wait()
        pltpu.make_async_copy(state_in, state_in, st2_send).wait()

    pltpu.make_async_copy(counts.at[pl.ds(1, 31)], counts.at[pl.ds(1, 31)], cnt_send).wait()

    pltpu.make_async_copy(kv.at[pl.ds(1, 16)], kv.at[pl.ds(1, 16)], kv_send).wait()


def per_device(
    segment_ids, attn_query, attention_keys, attention_values, attn_gate, delta_query, delta_key,
    update_rule_payload, delta_beta, delta_decay, delta_gate, norm_gain,
):
    entry = np.arange(128)
    freq = np.where(
        entry < ROTARY_ENTRIES, ROPE_THETA ** (-2.0 * (entry % 32) / ROTARY_ENTRIES), 0.0
    ).astype(np.float32)[None]
    vmem = pl.BlockSpec(memory_space=pltpu.VMEM)
    hbm = pl.BlockSpec(memory_space=pl.ANY)
    dma = pltpu.SemaphoreType.DMA
    wide = pltpu.VMEM((ROWS, 2048), BF16)
    return pl.pallas_call(
        kernel,
        out_shape=(wide, wide),
        in_specs=[vmem, vmem, hbm, vmem, vmem, hbm, hbm, hbm, hbm, vmem, vmem, hbm, vmem],
        out_specs=(vmem, vmem),
        scratch_shapes=[
            pltpu.VMEM((8, 128), F32),
            pltpu.VMEM((RANKS, 8, 128), F32),
            pltpu.VMEM((SLOTS, 2, ROWS, HEAD_WIDTH), BF16),
            pltpu.VMEM((GROUPS, ROWS, 2 * PER), F32),
            pltpu.VMEM((GROUPS, ROWS, 2 * PER), F32),
            pltpu.VMEM((HEADS_V, ROWS), F32),
            pltpu.VMEM((HEADS_V, 2 * DK, DK), BF16),
            pltpu.VMEM((HEADS_V, ROWS, DK), BF16),
            pltpu.VMEM((HEADS_V, ROWS, DK), F32),
            pltpu.VMEM((CHIPS, 2 * DK, DK), BF16),
            pltpu.VMEM((CHIPS, DK, DK), BF16),
            pltpu.VMEM((HEADS_V, DK, DK), BF16),
            pltpu.VMEM((HEADS_Q, ROWS, HEAD_WIDTH), BF16),
            pltpu.VMEM((SLOTS, ROWS, ROWS), F32),
            pltpu.VMEM((SLOTS, ROWS, ROWS), F32),
            pltpu.VMEM((ROWS, 128), F32),
            pltpu.VMEM((ROWS, 128), F32),
            pltpu.VMEM((SLOTS, ROWS, ROWS), F32),
            pltpu.VMEM((DK, DK), F32),
            pltpu.VMEM((HEADS_V, 2 * DK, DK), BF16),
            pltpu.VMEM((HEADS_V, 2 * DK, DK), BF16),
            dma, dma((2,)), dma, dma((SLOTS, 2)), dma, dma((GROUPS,)), dma, dma, dma, dma, dma, dma,
            pltpu.VMEM((ROWS, 2048), BF16),
            pltpu.VMEM((ROWS, 2048), BF16),
            pltpu.VMEM((ROWS, 1024), BF16),
            pltpu.VMEM((ROWS, 1024), BF16),
            pltpu.VMEM((ROWS, 2048), BF16),
            pltpu.VMEM((ROWS, 2048), BF16),
            dma((6,)),
        ],
        compiler_params=pltpu.CompilerParams(
            collective_id=0, has_side_effects=True, vmem_limit_bytes=52 * 2**20
        ),
    )(
        segment_ids.reshape(1, ROWS), freq,
        attn_query, attention_keys, attention_values, attn_gate, delta_query, delta_key,
        update_rule_payload, delta_beta.T, delta_decay.T, delta_gate, norm_gain.reshape(1, DK),
    )


def solution(mesh):
    rows = P(("dp", "ctx"))
    wide = P(("dp", "ctx"), None)
    return jax.shard_map(
        per_device,
        mesh=mesh,
        in_specs=(rows,) + (wide,) * 10 + (P(),),
        out_specs=(wide, wide),
        check_vma=False,
    )
```

```python
import jax
import jax.numpy as jnp
import numpy as np
from jax import lax
from jax.experimental import pallas as pl
from jax.experimental.pallas import tpu as pltpu
from jax.sharding import PartitionSpec as P

HEAD_WIDTH = 256
ROTARY_ENTRIES = 64
ROPE_THETA = 10000000.0
DK = 128
DOCS = 8
ROWS = 256
RANKS = 32
SLOTS = 17
HEADS_Q = 8
HEADS_K = 8
HEADS_V = 16
GROUPS = 4
PER = HEADS_K // GROUPS
MESH = pl.DeviceIdType.MESH
F32 = jnp.float32
BF16 = jnp.bfloat16
NEG = -1e30
LOG2E = 1.4426950408889634
CHIPS = 16
KEY, VALUE = 0, 1


def nn(a, b):
    return lax.dot_general(a, b, (((1,), (0,)), ((), ())), preferred_element_type=F32)


def nt(a, b):
    return lax.dot_general(a, b, (((1,), (1,)), ((), ())), preferred_element_type=F32)


def tn(a, b):
    return lax.dot_general(a, b, (((0,), (0,)), ((), ())), preferred_element_type=F32)


def iota(shape, dim):
    return lax.broadcasted_iota(jnp.int32, shape, dim)


def lanes(index, width):
    return pl.ds(pl.multiple_of(index * width, width), width)


def rotate(x, cos, sin):
    lane = iota(x.shape, 1)
    swapped = jnp.where(lane < 32, pltpu.roll(x, 96, 1), pltpu.roll(x, 32, 1))
    return x * cos + swapped * sin


def pair_diag(packed):
    zero = jnp.zeros((128, 128), packed.dtype)
    return jnp.concatenate(
        [
            jnp.concatenate([packed[:, :128], zero], axis=1),
            jnp.concatenate([zero, packed[:, 128:]], axis=1),
        ],
        axis=0,
    )


def inverses(lowers):
    row = iota((128, 256), 0)
    col = iota((128, 256), 1) % 128
    apart = row ^ col
    packed = [jnp.concatenate([x[:128, :128], x[128:, 128:]], axis=1) for x in lowers]
    inv = [jnp.where(apart == 0, 1.0, 0.0) - jnp.where(apart == 1, x, 0.0) for x in packed]
    block = 2
    while block < 128:
        here = (apart >= block) & (apart < 2 * block)
        off = [jnp.where(here, x, 0.0).astype(BF16) for x in packed]
        inv_b = [x.astype(BF16) for x in inv]
        left = [nn(x, pair_diag(c)) for x, c in zip(inv_b, off)]
        inv = [x - nn(c.astype(BF16), pair_diag(b)) for x, c, b in zip(inv, left, inv_b)]
        block *= 2
    inv_b = [x.astype(BF16) for x in inv]
    half = [nn(x[128:, :128].astype(BF16), b[:, :128]) for x, b in zip(lowers, inv_b)]
    corner = [nn(b[:, 128:], c.astype(BF16)) for b, c in zip(inv_b, half)]
    return [
        jnp.concatenate(
            [
                jnp.concatenate([b[:, :128], jnp.zeros((128, 128), BF16)], axis=1),
                jnp.concatenate([(-c).astype(BF16), b[:, 128:]], axis=1),
            ],
            axis=0,
        )
        for b, c in zip(inv_b, corner)
    ]


def kernel(
    seg_row, freq, q_hbm, k, v, gate_hbm, dq_hbm, dk_hbm, pv_hbm, beta, decay, dgate_hbm, gain,
    attn_out, delta_out,
    cnt, counts, kv, colg, colb, row_pack, mta, reach, intra, inbox, stage, state_in,
    qr, s_even, s_odd, top_even, top_odd, bias, state, twin, comb,
    cnt_send, cnt_recv, kv_send, kv_recv, twin_send, twin_recv, comb_send, comb_recv,
    st_send, st_recv, st2_send, st2_recv,
    q, gate, dq, dk, pv, dgate, in_sem, open_attn, open_delta,
):
    me = lax.axis_index("ctx")
    core = lax.rem(me, 2)
    chip = me // 2
    y = lax.rem(chip, 4)
    z = chip // 4

    def at(zz, yy, cc):
        return {"ctx": (lax.rem(zz, 4) * 4 + lax.rem(yy, 4)) * 2 + cc}

    barrier = pltpu.get_barrier_semaphore()

    @pl.loop(1, RANKS)
    def _(j):
        pl.semaphore_signal(
            barrier, inc=1, device_id={"ctx": lax.rem(me + j, RANKS)}, device_id_type=MESH
        )

    loads = [
        pltpu.make_async_copy(src, dst, in_sem.at[n])
        for n, (src, dst) in enumerate(
            [(q_hbm, q), (dq_hbm, dq), (dk_hbm, dk), (pv_hbm, pv), (gate_hbm, gate), (dgate_hbm, dgate)]
        )
    ]
    for load in loads:
        load.start()

    doc = iota((DOCS, ROWS), 0)
    mine = jnp.sum(jnp.where(seg_row[...] == doc, 1.0, 0.0), axis=1, keepdims=True)
    cnt[...] = jnp.broadcast_to(mine, (DOCS, 128))
    counts[0] = jnp.broadcast_to(mine, (DOCS, 128))
    lane1 = iota((ROWS, 128), 1)
    slot = (me * ROWS).astype(F32) + iota((ROWS, 1), 0).astype(F32)
    angle = slot * freq[...]
    cos = jnp.cos(angle)
    sin = jnp.sin(angle) * jnp.where(lane1 < 32, -1.0, 1.0)
    kv[0, KEY, :, :128] = rotate(k[:, :128].astype(F32), cos, sin).astype(BF16)
    kv[0, KEY, :, 128:] = k[:, 128:]
    kv[0, VALUE] = v[...]
    pl.semaphore_wait(barrier, RANKS - 1)

    def send_kv(part, src, dst, target):
        pltpu.make_async_remote_copy(
            kv.at[src, part], kv.at[dst, part], kv_send, kv_recv.at[dst, part],
            device_id=target, device_id_type=MESH,
        ).start()

    def got_kv(part, j):
        pltpu.make_async_copy(kv.at[j, part], kv.at[j, part], kv_recv.at[j, part]).wait()

    def to_twin(part, d):
        send_kv(part, 2 * d, 2 * d + 1 - 2 * core, at(z, y, 1 - core))

    def send_above(part):
        send_kv(part, 0, 8, at(z + 1, y, core))

    def send_own(part):
        for m in (1, 3, 2):

            @pl.when(y + m < 4)
            def _():
                send_kv(part, 0, 2 * m, at(z, y + m, core))

        @pl.when(core == 0)
        def _():
            to_twin(part, 0)

    def slot_of(source, m):
        return 2 * (4 + m - 4 * ((source + m) // 4))

    hop = (3, 1)
    behind = [lax.rem(y + 4 - t, 4) for t in hop]
    passed = [slot_of(b, t) for b, t in zip(behind, hop)]

    def relay_above(part):
        got_kv(part, 8)
        for m in (1, 3):
            send_kv(part, 8, slot_of(y, m), at(z, y + m, core))
        to_twin(part, 4)

    def relay_second(part):
        got_kv(part, 16)
        for m in (3, 1, 2):

            @pl.when(y + m >= 4)
            def _():
                send_kv(part, 16, 2 * (m + 4), at(z, y + m, core))

        @pl.when(core == 1)
        def _():
            to_twin(part, 8)

    def relay_passed(part):
        got_kv(part, passed[part])
        send_kv(part, passed[part], slot_of(behind[part], 2), at(z, y + hop[part], core))
        to_twin(part, passed[part] // 2)

    def relay_rest(part):
        for d in (1, 2, 3, 5, 6, 7):

            @pl.when(passed[part] != 2 * d)
            def _():
                got_kv(part, 2 * d)
                to_twin(part, d)

    def relay_last():
        for d in range(8):
            got_kv(KEY, 2 * d + 1)
            got_kv(VALUE, 2 * d + 1)

    @pl.loop(1, RANKS)
    def _(j):
        pltpu.make_async_remote_copy(
            cnt, counts.at[j], cnt_send, cnt_recv.at[jnp.minimum(j - 1, 1)],
            device_id={"ctx": lax.rem(me + j, RANKS)}, device_id_type=MESH,
        ).start()

    send_above(VALUE)
    send_above(KEY)
    send_own(VALUE)
    send_own(KEY)
    sums_of = jnp.where(iota((ROWS, ROWS), 0) <= iota((ROWS, ROWS), 1), 1.0, 0.0).astype(BF16)
    dec = decay[...]
    hi = dec.astype(BF16)
    mid = (dec - hi.astype(F32)).astype(BF16)
    low = (dec - hi.astype(F32) - mid.astype(F32)).astype(BF16)
    sums = nn(hi, sums_of) + nn(mid, sums_of) + nn(low, sums_of)
    row_pack[...] = sums
    seg_f = seg_row[...].astype(F32)
    pack = jnp.concatenate(
        [
            sums, beta[...],
            jnp.broadcast_to(seg_f, (96, ROWS)),
        ],
        axis=0,
    )
    columns = pack.T
    seg = columns[:, 32:33].astype(jnp.int32)
    for g in range(GROUPS):
        w = 2 * PER
        colg[g, :, :w] = columns[:, g * w : (g + 1) * w]
        colb[g, :, :w] = columns[:, 16 + g * w : 16 + (g + 1) * w]

    relay_above(VALUE)
    send_kv(VALUE, 0, 16, at(z + 2, y, core))
    send_kv(KEY, 0, 16, at(z + 2, y, core))

    loads[0].wait()
    for h in range(HEADS_Q):
        base = h * HEAD_WIDTH
        qr[h, :, :128] = rotate(q[:, base : base + 128].astype(F32), cos, sin).astype(BF16)
        qr[h, :, 128:] = q[:, base + 128 : base + 256]

    pltpu.make_async_copy(counts.at[1], counts.at[1], cnt_recv.at[0]).wait()
    held = jnp.where(counts[1] > 0.0, iota((DOCS, 128), 0).astype(F32), -1.0)
    held = jnp.where(me > 0, jnp.max(held, axis=0, keepdims=True), -1.0)
    first_doc = jnp.where(seg.astype(F32) == held[:, :1], 1.0, 0.0)
    row2 = iota((ROWS, ROWS), 0)
    col2 = iota((ROWS, ROWS), 1)
    same = (seg == seg_row[...]) & (row2 >= col2)
    seg_last = seg[ROWS - 1 : ROWS, :]
    last_doc = jnp.where(seg == seg_last, 1.0, 0.0)
    eye = jnp.where(iota((DK, DK), 0) == iota((DK, DK), 1), 1.0, 0.0)

    relay_above(KEY)

    def group(g):
        parts = []
        for i in range(PER):
            kh = g * PER + i
            kr = dk[:, lanes(kh, DK)]
            qx = dq[:, lanes(kh, DK)]
            kf = kr.astype(F32)
            qf = qx.astype(F32)
            rk = lax.rsqrt(jnp.sum(kf * kf, axis=1, keepdims=True) + 1e-06)
            rq = lax.rsqrt(jnp.sum(qf * qf, axis=1, keepdims=True) + 1e-06) * DK ** (-0.5)
            rk_row = jnp.broadcast_to(rk, (ROWS, 128)).T[0:1]
            gram = nt(kr, kr) * (rk * rk_row)
            probe = nt(qx, kr) * (rq * rk_row)
            for n in range(2):
                gc = colg[g][:, 2 * i + n : 2 * i + n + 1]
                bc = colb[g][:, 2 * i + n : 2 * i + n + 1]
                gr = row_pack[pl.ds(2 * kh + n, 1), :]
                span = jnp.where(same, jnp.exp(jnp.minimum(gc - gr, 0.0)), 0.0)
                parts.append((2 * kh + n, kf * rk, qf * rq, gc, bc, (span * gram) * bc, (span * probe).astype(BF16)))
        solved = inverses([p[5] for p in parts])

        @pl.when(g == 0)
        def _():
            relay_passed(VALUE)

        @pl.when(g == 1)
        def _():
            relay_passed(KEY)

        wus = []
        for (h, kn, qn, gc, bc, _, _), inv in zip(parts, solved):
            entry = first_doc * jnp.exp(gc)
            vf = pv[:, lanes(h, DK)].astype(F32)
            right = jnp.concatenate([kn * (bc * entry), vf * bc], axis=1).astype(BF16)
            wus.append(nn(inv, right).astype(BF16))
        inners = [nn(p[6], wu) for p, wu in zip(parts, wus)]
        boths = []
        for (h, kn, qn, gc, bc, _, _), wu in zip(parts, wus):
            tail = last_doc * jnp.exp(jnp.minimum(gc[ROWS - 1 : ROWS] - gc, 0.0))
            boths.append(tn(wu, (kn * tail).astype(BF16)))
        for (h, kn, qn, gc, bc, _, _), inner, both in zip(parts, inners, boths):
            entry = first_doc * jnp.exp(gc)
            reach[h] = (qn * entry - inner[:, :DK]).astype(BF16)
            intra[h] = inner[:, DK:]
            mt = eye * entry[ROWS - 1 : ROWS] - both[:DK]
            mta[h] = jnp.concatenate([mt, both[DK:]], axis=0).astype(BF16)

    heads = 2 * PER

    def send_heads(g):
        @pl.when(core == 0)
        def _():
            pltpu.make_async_remote_copy(
                mta.at[pl.ds(g * heads, heads)], twin.at[pl.ds(g * heads, heads)],
                twin_send, twin_recv.at[g],
                device_id={"ctx": me + 1}, device_id_type=MESH,
            ).start()

        @pl.when(core == 1)
        def _():
            pltpu.make_async_copy(
                twin.at[pl.ds(g * heads, heads)], twin.at[pl.ds(g * heads, heads)], twin_recv.at[g]
            ).wait()

            hs = [g * heads + i for i in range(heads)]
            pairs = [nn(twin[h], mta[h, :DK]) for h in hs]
            for h, both in zip(hs, pairs):
                comb[h, :DK] = both[:DK].astype(BF16)
                comb[h, DK:] = (both[DK:] + mta[h, DK:].astype(F32)).astype(BF16)
            for h in hs:
                pltpu.make_async_remote_copy(
                    comb.at[h], inbox.at[lax.rem(chip - h + CHIPS, CHIPS)], comb_send, comb_recv,
                    device_id={"ctx": 2 * h}, device_id_type=MESH,
                ).start()

    for load in loads[1:4]:
        load.wait()

    @pl.loop(0, GROUPS)
    def _(g):
        group(g)

        @pl.when(g == 0)
        def _():
            relay_second(VALUE)

        @pl.when(g == 1)
        def _():
            relay_second(KEY)

        @pl.when(g == 2)
        def _():
            relay_rest(VALUE)

        @pl.when(g == 3)
        def _():
            relay_rest(KEY)

        send_heads(g)

    pltpu.make_async_copy(
        counts.at[pl.ds(2, RANKS - 2)], counts.at[pl.ds(2, RANKS - 2)], cnt_recv.at[1]
    ).wait()
    totals = jnp.sum(counts[...], axis=0)
    totals = jnp.concatenate([totals, totals], axis=1)
    start_row = jnp.sum(jnp.where(doc < seg_row[...], totals, 0.0), axis=0, keepdims=True)
    starts = jnp.broadcast_to(start_row, (128, ROWS)).T[:, :1]
    pos0 = iota((ROWS, ROWS), 1).astype(F32)
    for j in range(SLOTS):
        allowed = (pos0 + ((me - j) * ROWS).astype(F32)) >= starts
        if j == 0:
            allowed = allowed & (row2 >= col2)
        bias[j] = jnp.where(allowed, 0.0, NEG)

    def overlap(low, now, now_top, later, later_top):
        nxt = jnp.minimum(low + 1, HEADS_Q - 1)
        best = total = acc = None
        if now is not None:
            top = now_top[...]
            top = jnp.concatenate([top, top], axis=1)
        for j in range(SLOTS):
            if later is not None:
                s = nt(qr[nxt], kv[j, 0]) + bias[j]
                later[j] = s
                m2 = jnp.maximum(s[:, :128], s[:, 128:])
                best = m2 if best is None else jnp.maximum(best, m2)
            if now is not None:
                w = jnp.exp2((now[j] - top) * (LOG2E * HEAD_WIDTH ** (-0.5)))
                t2 = w[:, :128] + w[:, 128:]
                total = t2 if total is None else total + t2
                part = nn(w.astype(BF16), kv[j, 1])
                acc = part if acc is None else acc + part
        if later is not None:
            later_top[...] = jnp.broadcast_to(jnp.max(best, axis=1, keepdims=True), (ROWS, 128))
        if now is not None:
            total = jnp.sum(total, axis=1, keepdims=True)
            attn_out[:, lanes(low, HEAD_WIDTH)] = (
                acc * (1.0 / total) * open_attn[low]
            ).astype(BF16)

    def two_heads(i):
        overlap(2 * i, s_even, top_even, s_odd, top_odd)
        overlap(2 * i + 1, s_odd, top_odd, s_even, top_even)

    loads[4].wait()
    loads[5].wait()

    @pl.loop(0, HEADS_Q)
    def _(h):
        open_attn[h] = jax.nn.sigmoid(gate[:, lanes(h, HEAD_WIDTH)].astype(F32))
        for i in range(2):
            gt = dgate[:, lanes(2 * h + i, DK)].astype(F32)
            open_delta[2 * h + i] = gain[...] * (gt * jax.nn.sigmoid(gt))

    relay_last()
    overlap(-1, None, None, s_even, top_even)

    @pl.loop(0, 4)
    def _(i):
        two_heads(i)

        @pl.when((core == 0) & (i == 1))
        def _():
            pltpu.make_async_copy(inbox, inbox, comb_recv).wait()
            state[...] = jnp.zeros((DK, DK), F32)

            @pl.loop(0, CHIPS)
            def _(c):
                j = lax.rem(c - chip + CHIPS, CHIPS)
                stage[j] = state[...].astype(BF16)
                state[...] = nn(stage[j], inbox[j, :DK]) + inbox[j, DK:].astype(F32)

                pltpu.make_async_remote_copy(
                    stage.at[j], state_in.at[chip], st2_send, st2_recv,
                    device_id={"ctx": 2 * c + 1}, device_id_type=MESH,
                ).start()

                @pl.when(j != 0)
                def _():
                    pltpu.make_async_remote_copy(
                        stage.at[j], state_in.at[chip], st_send, st_recv,
                        device_id={"ctx": 2 * c}, device_id_type=MESH,
                    ).start()

                @pl.when(j == 0)
                def _():
                    state_in[chip] = stage[0]

    @pl.when(core == 0)
    def _():
        pltpu.make_async_copy(state_in.at[pl.ds(0, 15)], state_in.at[pl.ds(0, 15)], st_recv).wait()

    @pl.when(core == 1)
    def _():
        pltpu.make_async_copy(state_in, state_in, st2_recv).wait()

        @pl.loop(0, HEADS_V // 8)
        def _(t):
            hs = [8 * t + i for i in range(8)]
            moved = [nn(state_in[h], twin[h, :DK]) + twin[h, DK:].astype(F32) for h in hs]
            for h, later in zip(hs, moved):
                state_in[h] = later.astype(BF16)

        pltpu.make_async_copy(comb, comb, comb_send).wait()

    @pl.loop(0, HEADS_V // 4)
    def _(t):
        for i in range(4):
            h = 4 * t + i
            out = intra[h] + nt(reach[h], state_in[h])
            spread = lax.rsqrt(jnp.mean(out * out, axis=1, keepdims=True) + 1e-06)
            res = out * spread * open_delta[h]
            delta_out[:, lanes(h, DK)] = res.astype(BF16)

    @pl.when(core == 0)
    def _():
        pltpu.make_async_copy(mta, mta, twin_send).wait()
        pltpu.make_async_copy(stage.at[pl.ds(1, 15)], stage.at[pl.ds(1, 15)], st_send).wait()
        pltpu.make_async_copy(state_in, state_in, st2_send).wait()

    pltpu.make_async_copy(counts.at[pl.ds(1, 31)], counts.at[pl.ds(1, 31)], cnt_send).wait()

    pltpu.make_async_copy(kv.at[pl.ds(1, 16)], kv.at[pl.ds(1, 16)], kv_send).wait()


def per_device(
    segment_ids, attn_query, attention_keys, attention_values, attn_gate, delta_query, delta_key,
    update_rule_payload, delta_beta, delta_decay, delta_gate, norm_gain,
):
    entry = np.arange(128)
    freq = np.where(
        entry < ROTARY_ENTRIES, ROPE_THETA ** (-2.0 * (entry % 32) / ROTARY_ENTRIES), 0.0
    ).astype(np.float32)[None]
    vmem = pl.BlockSpec(memory_space=pltpu.VMEM)
    hbm = pl.BlockSpec(memory_space=pl.ANY)
    dma = pltpu.SemaphoreType.DMA
    wide = pltpu.VMEM((ROWS, 2048), BF16)
    return pl.pallas_call(
        kernel,
        out_shape=(wide, wide),
        in_specs=[vmem, vmem, hbm, vmem, vmem, hbm, hbm, hbm, hbm, vmem, vmem, hbm, vmem],
        out_specs=(vmem, vmem),
        scratch_shapes=[
            pltpu.VMEM((8, 128), F32),
            pltpu.VMEM((RANKS, 8, 128), F32),
            pltpu.VMEM((SLOTS, 2, ROWS, HEAD_WIDTH), BF16),
            pltpu.VMEM((GROUPS, ROWS, 2 * PER), F32),
            pltpu.VMEM((GROUPS, ROWS, 2 * PER), F32),
            pltpu.VMEM((HEADS_V, ROWS), F32),
            pltpu.VMEM((HEADS_V, 2 * DK, DK), BF16),
            pltpu.VMEM((HEADS_V, ROWS, DK), BF16),
            pltpu.VMEM((HEADS_V, ROWS, DK), F32),
            pltpu.VMEM((CHIPS, 2 * DK, DK), BF16),
            pltpu.VMEM((CHIPS, DK, DK), BF16),
            pltpu.VMEM((HEADS_V, DK, DK), BF16),
            pltpu.VMEM((HEADS_Q, ROWS, HEAD_WIDTH), BF16),
            pltpu.VMEM((SLOTS, ROWS, ROWS), F32),
            pltpu.VMEM((SLOTS, ROWS, ROWS), F32),
            pltpu.VMEM((ROWS, 128), F32),
            pltpu.VMEM((ROWS, 128), F32),
            pltpu.VMEM((SLOTS, ROWS, ROWS), F32),
            pltpu.VMEM((DK, DK), F32),
            pltpu.VMEM((HEADS_V, 2 * DK, DK), BF16),
            pltpu.VMEM((HEADS_V, 2 * DK, DK), BF16),
            dma, dma((2,)), dma, dma((SLOTS, 2)), dma, dma((GROUPS,)), dma, dma, dma, dma, dma, dma,
            pltpu.VMEM((ROWS, 2048), BF16),
            pltpu.VMEM((ROWS, 2048), BF16),
            pltpu.VMEM((ROWS, 1024), BF16),
            pltpu.VMEM((ROWS, 1024), BF16),
            pltpu.VMEM((ROWS, 2048), BF16),
            pltpu.VMEM((ROWS, 2048), BF16),
            dma((6,)),
            pltpu.VMEM((HEADS_Q, ROWS, HEAD_WIDTH), F32),
            pltpu.VMEM((HEADS_V, ROWS, DK), F32),
        ],
        compiler_params=pltpu.CompilerParams(
            collective_id=0, has_side_effects=True, vmem_limit_bytes=52 * 2**20
        ),
    )(
        segment_ids.reshape(1, ROWS), freq,
        attn_query, attention_keys, attention_values, attn_gate, delta_query, delta_key,
        update_rule_payload, delta_beta.T, delta_decay.T, delta_gate, norm_gain.reshape(1, DK),
    )


def solution(mesh):
    rows = P(("dp", "ctx"))
    wide = P(("dp", "ctx"), None)
    return jax.shard_map(
        per_device,
        mesh=mesh,
        in_specs=(rows,) + (wide,) * 10 + (P(),),
        out_specs=(wide, wide),
        check_vma=False,
    )
```
